128 devices in a mesh: wave: 64 (over z, y, x_lo, core), lev: 2 (over x_hi).
Axes of the slice: x: 4 (x_hi: 2, x_lo: 2; x = x_hi * 2 + x_lo), y: 4, z: 4, core: 2. Of those that a mesh axis runs over, the one named last changes fastest.
Arguments:
- spectra: bfloat16 [25600, 6, 3072], P('wave', None, 'lev'), may hold values from -0.4375 to 0.4375
- legendre: bfloat16 [25600, 64, 128], P('wave'), may hold values from -0.15625 to 0.15625
- block_slot: int32 [25600], P('wave'), may hold values from 0 to 20, as said below
- wavenumber: int32 [1280], replicated, may hold values from 0 to 1279, as said below
- cycle_points: int32 [128], P('wave'), may hold values from 20 to 5136, as said below
- quad_weight: float32 [128], P('wave'), may hold values from 0.02 to 0.2
Outputs:
- spectral_tendency: bfloat16 [25600, 6, 3072], P('wave', None, 'lev')
- grid_fields: bfloat16 [128, 3, 246528], P('wave', None, 'lev')
The draws below stay inside these ranges and needn't reach their ends.
Inputs may be any that keep to these rules, and one draw needn't show every extreme that they name: `wavenumber`: A permutation of 0 .. 1279; slots d * 20 to (d + 1) * 20 - 1 belong to index d of wave, and one index holds the wavenumbers 0 .. 19. `block_slot`: among the 400 entries of one index of wave, each local slot whose wavenumber is m appears exactly 20 - m // 64 times, in any order; the other entries are 20; on the index that holds wavenumbers 0 .. 19 there are none. `cycle_points`: each value is 4 j + 20 for a cycle index j from the pole; some cycle has 5136 points and some 20.
All inputs are finite; a program needn't handle non-finite values.
Results may differ from the reference program's by a relative error of at most 0.008.
Values may be sent and summed in bfloat16 or wider, within the bound.
No kernel may reach another device: no remote copies, remote signals or barrier semaphores. Data moves between devices by JAX's collectives and lax.ppermute only.
A program may use at most 320 MiB of HBM per device.

```python
import math
import jax
import jax.numpy as jnp
from jax import lax

MMAX = 1280
NBLK = 64
M_DEV = 20
NBMAX = 20
NB_DEV = 400
NB_TOT = 25600
LEVELS = 48
NLAT_W = 128
NLON = 5136
N_WAVE = 64


def wavenumber_lists(key):
    devices = MMAX // M_DEV
    key_heavy, key_remaining, key_lowest, key_shuffle = jax.random.split(key, 4)
    heavy_index = jax.random.randint(key_heavy, (), 0, devices)
    remaining = jax.random.permutation(key_remaining, MMAX - M_DEV) + M_DEV
    lowest = jax.random.permutation(key_lowest, M_DEV)
    stacked = jnp.concatenate([lowest, remaining]).reshape(devices, M_DEV)
    rotation = (jnp.arange(devices) - heavy_index) % devices
    numbers = stacked[rotation].astype(jnp.int32)
    counts = NBMAX - numbers // NBLK
    block_ends = jnp.cumsum(counts, axis=1)
    position = jnp.arange(NB_DEV, dtype=jnp.int32)
    slots = jnp.sum((block_ends[:, None, :] <= position[None, :, None]).astype(jnp.int32), axis=2)
    row_keys = jax.random.split(key_shuffle, devices)
    shuffled = jax.vmap(jax.random.permutation)(row_keys, slots)
    return (numbers.reshape(MMAX).astype(jnp.int32), shuffled.reshape(NB_DEV * devices).astype(jnp.int32))


def draw_wavenumber(key, part):
    numbers, slots = wavenumber_lists(key)
    return numbers


def draw_block_slot(key, part):
    numbers, slots = wavenumber_lists(key)
    return slots


def draw_cycle_points(key, part):
    key = jax.random.fold_in(key, 5)
    key_cycles, key_chosen = jax.random.split(key)
    cycle_index = jax.random.randint(key_cycles, (NLAT_W,), 0, MMAX)
    counts = 20 + 4 * cycle_index
    chosen = jax.random.permutation(key_chosen, NLAT_W)
    counts = counts.at[chosen[0]].set(NLON)
    counts = counts.at[chosen[1]].set(20)
    return counts.astype(jnp.int32)


def levels(key, extent, pieces, least, top_value):
    level, own = 1.0, jax.random.fold_in(key, 6)
    for dim, shards_of in pieces:
        draws = jnp.exp(jax.random.uniform(jax.random.fold_in(own, dim), (shards_of,), jnp.float32, least / len(pieces), top_value / len(pieces)))
        level = level * jnp.repeat(draws, extent[dim] // shards_of).reshape([-1 if axis == dim else 1 for axis in range(len(extent))])
    return level


def centred(key, extent, width, most, cuts=(), held_as=jnp.bfloat16):
    entries = jax.random.normal(key, extent, jnp.float32) * width
    if len(cuts) > 0:
        entries = levels(key, extent, cuts, -0.22, 0.18) * entries
    return jnp.clip(entries, min=-most, max=most).astype(held_as)


def setup_inputs(seed: int = 0) -> dict:
    splits = jax.random.split(jax.random.key(seed), 7)
    return {
        "spectra": centred(splits[0], (NB_TOT, 6, LEVELS * NBLK), 0.03, 0.4375, ((0, 64), (2, 2))),
        "legendre": centred(splits[1], (NB_TOT, NBLK, NLAT_W), MMAX ** -0.5, 0.15625, ((0, 64),)),
        "block_slot": draw_block_slot(jax.random.fold_in(splits[6], 71), 0),
        "wavenumber": draw_wavenumber(jax.random.fold_in(splits[6], 71), 0),
        "cycle_points": draw_cycle_points(jax.random.fold_in(splits[6], 71), 0),
        "quad_weight": jnp.clip(jnp.exp(math.log(0.2) - 2.3025851 * jax.random.uniform(splits[5], (NLAT_W,), jnp.float32) ** levels(splits[5], (NLAT_W,), ((0, 64),), -0.2, 0.2)), 0.02, 0.2),
    }


def fourier_tables(points, wavenumber, columns):
    phases = (wavenumber[None, :] * columns[:, None]) % points
    angles = phases.astype(jnp.float32) * (2.0 * math.pi / points.astype(jnp.float32))
    inside = (2 * wavenumber[None, :] < points) & (columns[:, None] < points)
    cosine = jnp.where(inside, jnp.cos(angles), 0.0)
    sine_part = jnp.where(inside, -jnp.sin(angles), 0.0)
    return cosine, sine_part


def inverse_table(points, wavenumber, columns):
    cosine, sine_part = fourier_tables(points, wavenumber, columns)
    factor = jnp.where(wavenumber == 0, 1.0, 2.0).astype(jnp.float32)[None, :]
    return jnp.concatenate([cosine * factor, sine_part * factor], axis=1).astype(jnp.bfloat16)


def forward_table(points, wavenumber, columns):
    cosine, sine_part = fourier_tables(points, wavenumber, columns)
    return jnp.concatenate([cosine, sine_part], axis=1).astype(jnp.bfloat16)


def reference(spectra, legendre, block_slot, wavenumber, cycle_points, quad_weight):
    channels = 6 * LEVELS
    spec_groups = spectra.reshape(N_WAVE, NB_DEV, 6, LEVELS, NBLK)
    leg_groups = legendre.reshape(N_WAVE, NB_DEV, NBLK, NLAT_W)
    slot_groups = block_slot.reshape(N_WAVE, NB_DEV)
    slot_ids = jnp.arange(M_DEV, dtype=jnp.int32)

    def synthesis(group):
        spec_part, leg_part, slot_part = group
        products = jnp.einsum("knj,kcln->kjcl", leg_part.astype(jnp.float32), spec_part.astype(jnp.float32), precision=lax.Precision.HIGHEST)
        onehot = (slot_part[:, None] == slot_ids[None, :]).astype(jnp.float32)
        return jnp.einsum("ks,kjcl->sjcl", onehot, products, precision=lax.Precision.HIGHEST)

    fourier = lax.map(synthesis, (spec_groups, leg_groups, slot_groups))
    fourier = fourier.reshape(MMAX, NLAT_W, channels).astype(jnp.bfloat16)
    columns = jnp.arange(NLON, dtype=jnp.int32)

    def cycle(index):
        points = cycle_points[index]
        column_part = lax.dynamic_index_in_dim(fourier, index, 1, keepdims=False)
        stacked = column_part.reshape(MMAX, 2, 3 * LEVELS)
        stacked = jnp.concatenate([stacked[:, 0, :], stacked[:, 1, :]], axis=0)
        grid_cycle = jnp.dot(inverse_table(points, wavenumber, columns), stacked, preferred_element_type=jnp.float32).astype(jnp.bfloat16)
        values = grid_cycle.astype(jnp.float32).reshape(NLON, 3, LEVELS)
        flux_terms = jnp.stack([values[:, 0] * values[:, 2], values[:, 1] * values[:, 2], 0.5 * values[:, 2] * values[:, 2]], axis=1)
        flux_terms = flux_terms.reshape(NLON, 3 * LEVELS).astype(jnp.bfloat16)
        sums = jnp.dot(forward_table(points, wavenumber, columns).T, flux_terms, preferred_element_type=jnp.float32) * quad_weight[index]
        packed = jnp.stack([sums[:MMAX], sums[MMAX:]], axis=1).reshape(MMAX, channels)
        grid_out = jnp.transpose(grid_cycle.reshape(NLON, 3, LEVELS), (1, 0, 2)).reshape(3, NLON * LEVELS)
        return grid_out, packed.astype(jnp.bfloat16)

    grid_fields, returned = lax.map(cycle, jnp.arange(NLAT_W, dtype=jnp.int32))
    returned = jnp.transpose(returned, (1, 0, 2)).reshape(N_WAVE, M_DEV, NLAT_W, channels)

    def analysis(group):
        coefficients, leg_part, slot_part = group
        extended = jnp.concatenate([coefficients, jnp.zeros((1, NLAT_W, channels), jnp.bfloat16)], axis=0)
        selected = extended[slot_part].reshape(NB_DEV, NLAT_W, 6, LEVELS)
        result = jnp.einsum("knj,kjcl->kcln", leg_part.astype(jnp.float32), selected.astype(jnp.float32), precision=lax.Precision.HIGHEST)
        return result.reshape(NB_DEV, 6, LEVELS * NBLK).astype(jnp.bfloat16)

    spectral_tendency = lax.map(analysis, (returned, leg_groups, slot_groups)).reshape(NB_TOT, 6, LEVELS * NBLK)
    return spectral_tendency, grid_fields
```

```python
import functools
import math

import jax
import jax.numpy as jnp
from jax import lax
from jax.experimental import pallas as pl
from jax.experimental.pallas import tpu as pltpu
from jax.sharding import PartitionSpec as P

MMAX = 1280
NLON = 5136
NBLK = 64
WAVES = 64
SLOTS = 20
HALF = NLON // 2
PAYLOAD = 2880
ROWS = 24
QUARTER = 1296
TILE = 432
FINE = 48
COARSE = QUARTER // FINE
OUTR = 336

f32 = jnp.float32
bf16 = jnp.bfloat16


def params(mib):
    return pltpu.CompilerParams(vmem_limit_bytes=mib * 1024 * 1024)


def block_diagonal(block):
    zero = jnp.zeros_like(block)
    return jnp.concatenate(
        [jnp.concatenate([block, zero], axis=1), jnp.concatenate([zero, block], axis=1)], axis=0
    )


def synthesis_kernel(slot_ref, spec_ref, leg_ref, out_ref, acc, stage, packed, rows, *, group):
    step = pl.program_id(0)

    @pl.when(step == 0)
    def _():
        acc[...] = jnp.zeros_like(acc)
        packed[...] = jnp.zeros_like(packed)

    blocks = spec_ref.shape[1]

    def body(g, carry):
        base = pl.multiple_of(g * group, group)
        for c in range(6):
            x = spec_ref[c, pl.ds(base, group), :].astype(f32)
            for t in range(12):
                stage[pl.ds(c * 12 + t, group, stride=72), :] = x[:, t * 128 : (t + 1) * 128]
        for kk in range(group):
            x = stage[kk * 72 : (kk + 1) * 72, :].astype(bf16)
            w = block_diagonal(leg_ref[base + kk])
            prod = jnp.dot(x, w, preferred_element_type=f32)
            slot = slot_ref[step * blocks + base + kk]
            acc[slot, 0:72, :] += prod[:, :128]
            acc[slot, 72:144, :] += prod[:, 128:]
        return carry

    lax.fori_loop(0, blocks // group, body, 0)

    @pl.when(step == pl.num_programs(0) - 1)
    def _():
        for q in range(SLOTS):
            for r in range(2):
                for l2 in range(2):
                    packed[pl.ds((q * 2 + r) * 72 + l2, 36, stride=2), :] = acc[
                        q, l2 * 72 + r * 36 : l2 * 72 + r * 36 + 36, :
                    ]
        for i in range(ROWS):
            rows[pl.ds(i, 128, stride=ROWS), :] = packed[i * 128 : (i + 1) * 128, :].T
        out_ref[...] = rows[...].astype(bf16)


def synthesis(block_slot, spec, legendre):
    count = spec.shape[1]
    blocks = 80
    group = 16
    return pl.pallas_call(
        functools.partial(synthesis_kernel, group=group),
        grid_spec=pltpu.PrefetchScalarGridSpec(
            num_scalar_prefetch=1,
            grid=(count // blocks,),
            in_specs=[
                pl.BlockSpec((6, blocks, 24 * NBLK), lambda i, s: (0, i, 0)),
                pl.BlockSpec((blocks, NBLK, 128), lambda i, s: (i, 0, 0)),
            ],
            out_specs=pl.BlockSpec((128 * ROWS, 128), lambda i, s: (0, 0)),
            scratch_shapes=[
                pltpu.VMEM((SLOTS + 1, 144, 128), f32),
                pltpu.VMEM((group * 72, 128), f32),
                pltpu.VMEM((ROWS * 128, 128), f32),
                pltpu.VMEM((ROWS * 128, 128), f32),
            ],
        ),
        out_shape=jax.ShapeDtypeStruct((128 * ROWS, 128), bf16),
        compiler_params=params(40),
        name="synthesis",
    )(block_slot, spec, legendre)


def analysis_kernel(slot_ref, in_ref, leg_ref, out_ref, coef, stage, packed, rows, *, group):
    step = pl.program_id(0)

    @pl.when(step == 0)
    def _():
        rows[...] = in_ref[...].astype(f32)
        for i in range(ROWS - 1):
            packed[i * 128 : (i + 1) * 128, :] = rows[pl.ds(i, 128, stride=ROWS), :].T
        for q in range(SLOTS):
            for l2 in range(2):
                for r in range(2):
                    stage[r * 36 : r * 36 + 36, :] = packed[
                        pl.ds((q * 2 + r) * 72 + l2, 36, stride=2), :
                    ]
                coef[q, 0:72, l2 * 128 : (l2 + 1) * 128] = stage[0:72, :].astype(bf16)
        coef[SLOTS] = jnp.zeros(coef.shape[1:], bf16)

    blocks = out_ref.shape[1]

    def body(g, carry):
        base = pl.multiple_of(g * group, group)
        for kk in range(group):
            slot = slot_ref[step * blocks + base + kk]
            w = block_diagonal(leg_ref[base + kk])
            stage[kk * 72 : (kk + 1) * 72, :] = lax.dot_general(
                coef[slot], w, (((1,), (1,)), ((), ())), preferred_element_type=f32
            )[:72]
        for c in range(6):
            for t in range(12):
                out_ref[c, pl.ds(base, group), t * 128 : (t + 1) * 128] = stage[
                    pl.ds(c * 12 + t, group, stride=72), :
                ].astype(bf16)
        return carry

    lax.fori_loop(0, blocks // group, body, 0)


def analysis(block_slot, payload, legendre):
    count = legendre.shape[0]
    blocks = 80
    group = 16
    return pl.pallas_call(
        functools.partial(analysis_kernel, group=group),
        grid_spec=pltpu.PrefetchScalarGridSpec(
            num_scalar_prefetch=1,
            grid=(count // blocks,),
            in_specs=[
                pl.BlockSpec((128 * ROWS, 128), lambda i, s: (0, 0)),
                pl.BlockSpec((blocks, NBLK, 128), lambda i, s: (i, 0, 0)),
            ],
            out_specs=pl.BlockSpec((6, blocks, 24 * NBLK), lambda i, s: (0, i, 0)),
            scratch_shapes=[
                pltpu.VMEM((SLOTS + 1, 80, 256), bf16),
                pltpu.VMEM((group * 72, 128), f32),
                pltpu.VMEM((ROWS * 128, 128), f32),
                pltpu.VMEM((ROWS * 128, 128), f32),
            ],
        ),
        out_shape=jax.ShapeDtypeStruct((6, count, 24 * NBLK), bf16),
        compiler_params=params(40),
        name="analysis",
    )(block_slot, payload, legendre)


def cosine_sine(phase, points, inverse):
    turns = jnp.floor(phase * inverse + 0.5)
    rest = phase - turns * points
    quarter = jnp.floor(4.0 * rest * inverse + 0.5)
    z = (4.0 * rest - quarter * points) * inverse * (0.5 * math.pi)
    z2 = z * z
    s = z * (1.0 + z2 * (-1 / 6 + z2 * (1 / 120 + z2 * (-1 / 5040 + z2 * (1 / 362880)))))
    c = 1.0 + z2 * (-0.5 + z2 * (1 / 24 + z2 * (-1 / 720 + z2 * (1 / 40320))))
    odd = jnp.abs(quarter) == 1.0
    flip = jnp.abs(quarter) == 2.0
    first = jnp.where(odd, s, c)
    second = jnp.where(odd, c, s)
    cos_sign = jnp.where(flip | (quarter == 1.0), -1.0, 1.0)
    sin_sign = jnp.where(flip | (quarter == -1.0), -1.0, 1.0)
    return first * cos_sign, second * sin_sign


def table_kernel(points_ref, m_ref, out_ref, fine_c, fine_s, coarse_c, coarse_s):
    step = pl.program_id(0)
    points = jnp.full((1, MMAX), points_ref[0], jnp.int32).astype(f32)
    inverse = 1.0 / points

    @pl.when(step == 0)
    def _():
        m = m_ref[...].astype(f32)
        live = jnp.where(2.0 * m < points, 1.0, 0.0)
        for base in range(0, FINE, 8):
            index = (base + lax.broadcasted_iota(jnp.int32, (8, MMAX), 0)).astype(f32)
            c, s = cosine_sine(index * m, points, inverse)
            fine_c[base : base + 8, :] = c
            fine_s[base : base + 8, :] = s
        for base in range(0, coarse_c.shape[0], 8):
            index = (FINE * (base + lax.broadcasted_iota(jnp.int32, (8, MMAX), 0))).astype(f32)
            c, s = cosine_sine(index * m, points, inverse)
            coarse_c[base : base + 8, :] = c * live
            coarse_s[base : base + 8, :] = s * live

    each = out_ref.shape[0] // FINE
    for b in range(each):
        row = step * each + b
        for lane in range(0, MMAX, 256):
            at = slice(lane, lane + 256)
            cb = coarse_c[pl.ds(row, 1), at]
            sb = coarse_s[pl.ds(row, 1), at]
            cf = fine_c[:, at]
            sf = fine_s[:, at]
            out_ref[b * FINE : (b + 1) * FINE, at] = (cb * cf - sb * sf).astype(bf16)
            out_ref[b * FINE : (b + 1) * FINE, MMAX + lane : MMAX + lane + 256] = (
                -(sb * cf + cb * sf)
            ).astype(bf16)


def tables(points, m_row):
    each = 3 * FINE
    return pl.pallas_call(
        table_kernel,
        grid_spec=pltpu.PrefetchScalarGridSpec(
            num_scalar_prefetch=1,
            grid=(QUARTER // each,),
            in_specs=[pl.BlockSpec((1, MMAX), lambda i, s: (0, 0))],
            out_specs=pl.BlockSpec((each, 2 * MMAX), lambda i, s: (i, 0)),
            scratch_shapes=[
                pltpu.VMEM((FINE, MMAX), f32),
                pltpu.VMEM((FINE, MMAX), f32),
                pltpu.VMEM((32, MMAX), f32),
                pltpu.VMEM((32, MMAX), f32),
            ],
        ),
        out_shape=jax.ShapeDtypeStruct((QUARTER, 2 * MMAX), bf16),
        compiler_params=params(24),
        name="tables",
    )(points, m_row)


def rotation(m):
    k = m & 3
    a = jnp.where(k == 0, 1.0, jnp.where(k == 2, -1.0, 0.0))
    b = jnp.where(k == 1, 1.0, jnp.where(k == 3, -1.0, 0.0))
    sign = jnp.where((k & 1) == 0, 1.0, -1.0)
    return a.astype(f32), b.astype(f32), sign.astype(f32)


def cycle_kernel(
    scalar_ref, weight_ref, in_ref, m_ref, table_ref, ret_ref, keep_ref, send_ref,
    rows, packed, coef, flux, grid,
):
    points = scalar_ref[0]
    lev = scalar_ref[1]
    quarter = points >> 2
    low = lax.broadcasted_iota(jnp.int32, (72, 128), 1) < 64

    rows[...] = in_ref[...].astype(f32)
    for i in range(ROWS - 1):
        block = jnp.concatenate(
            [
                rows[pl.ds(i, WAVES, stride=2 * ROWS), :],
                rows[pl.ds(ROWS + i, WAVES, stride=2 * ROWS), :],
            ],
            axis=0,
        )
        packed[i * 128 : (i + 1) * 128, :] = block.T

    for i in range(SLOTS // 2):
        lanes = slice(i * 128, (i + 1) * 128)
        m = m_ref[:, lanes]
        factor = jnp.where(m == 0, 1.0, 2.0).astype(f32)
        a, b, sign = rotation(m)
        parts = []
        for r in range(2):
            even = packed[(4 * i + r) * 72 : (4 * i + r + 1) * 72, :]
            odd = packed[(4 * i + 2 + r) * 72 : (4 * i + 3 + r) * 72, :]
            first = jnp.where(low, even, pltpu.roll(odd, 64, 1)) * factor
            second = jnp.where(low, pltpu.roll(even, 64, 1), odd) * factor
            parts.append((first, second))
        (re0, re1), (im0, im1) = parts
        for f in range(3):
            at = slice(f * 24, (f + 1) * 24)
            re = jnp.concatenate([re0[at], re1[at]], axis=0)
            im = jnp.concatenate([im0[at], im1[at]], axis=0)
            turned = [
                (re, im),
                (a * re - b * im, a * im + b * re),
                (sign * re, sign * im),
                (a * re + b * im, a * im - b * re),
            ]
            for r4 in range(4):
                out = slice(f * 192 + r4 * 48, f * 192 + (r4 + 1) * 48)
                coef[out, i * 128 : (i + 1) * 128] = turned[r4][0].astype(bf16)
                coef[out, MMAX + i * 128 : MMAX + (i + 1) * 128] = turned[r4][1].astype(bf16)

    tiles = QUARTER // TILE

    def inverse(step, carry):
        start = pl.multiple_of((tiles - 1 - step) * TILE, 16)
        values = lax.dot_general(
            table_ref[pl.ds(start, TILE), :], coef[...], (((1,), (1,)), ((), ())),
            preferred_element_type=f32,
        )
        index = start + lax.broadcasted_iota(jnp.int32, (TILE, 192), 0)
        fields = [
            jnp.where(index < quarter, values[:, f * 192 : (f + 1) * 192], 0.0)
            .astype(bf16)
            .astype(f32)
            for f in range(3)
        ]
        for f in range(3):
            for r4 in range(4):
                grid[f, pl.ds(r4 * quarter + start, TILE), 0:48] = fields[f][
                    :, r4 * 48 : (r4 + 1) * 48
                ]
        products = [fields[0] * fields[2], fields[1] * fields[2], 0.5 * fields[2] * fields[2]]
        for f in range(3):
            flux[step, f * 192 : (f + 1) * 192, :] = products[f].T.astype(bf16)
        return carry

    lax.fori_loop(0, tiles, inverse, 0)

    chunk = 48
    for which, ref in ((0, keep_ref), (1, send_ref)):
        half = lev if which == 0 else 1 - lev

        def place(j, carry, half=half, ref=ref):
            for f in range(3):
                pieces = []
                for s in range(8):
                    first = half * HALF + j * (8 * chunk) + s
                    piece = grid[f, pl.ds(first, chunk, stride=8), :][:, 0:48]
                    place_of = first + 8 * lax.broadcasted_iota(jnp.int32, (chunk, 48), 0)
                    pieces.append(jnp.where(place_of < points, piece, 0.0))
                ref[f, pl.ds(pl.multiple_of(j * chunk, 16), chunk), :] = jnp.concatenate(
                    pieces, axis=1
                ).astype(bf16)
            return carry

        lax.fori_loop(0, OUTR // chunk, place, 0)

    weight = weight_ref[0]

    def forward(n, carry):
        at = pl.multiple_of(n * 256, 256)
        cos_sum = jnp.zeros((576, 256), f32)
        sin_sum = jnp.zeros((576, 256), f32)
        for step in range(tiles):
            start = (tiles - 1 - step) * TILE
            cos_sum += jnp.dot(
                flux[step], table_ref[start : start + TILE, pl.ds(at, 256)],
                preferred_element_type=f32,
            )
            sin_sum += jnp.dot(
                flux[step], table_ref[start : start + TILE, pl.ds(at + MMAX, 256)],
                preferred_element_type=f32,
            )
        for i2 in range(2):
            lanes = slice(i2 * 128, (i2 + 1) * 128)
            a, b, sign = rotation(m_ref[:, pl.ds(at + i2 * 128, 128)])
            result = [[], []]
            for f in range(3):
                c = [cos_sum[f * 192 + r4 * 48 : f * 192 + (r4 + 1) * 48, lanes] for r4 in range(4)]
                s = [sin_sum[f * 192 + r4 * 48 : f * 192 + (r4 + 1) * 48, lanes] for r4 in range(4)]
                result[0].append(
                    (c[0] + sign * c[2] + a * (c[1] + c[3]) + b * (s[1] - s[3])) * weight
                )
                result[1].append(
                    (s[0] + sign * s[2] + a * (s[1] + s[3]) - b * (c[1] - c[3])) * weight
                )
            for r in range(2):
                first = jnp.concatenate([x[:24] for x in result[r]], axis=0)
                second = jnp.concatenate([x[24:] for x in result[r]], axis=0)
                row = pl.multiple_of((n * 8 + 4 * i2 + r) * 72, 8)
                packed[pl.ds(row, 72), :] = jnp.where(low, first, pltpu.roll(second, 64, 1))
                packed[pl.ds(row + 144, 72), :] = jnp.where(low, pltpu.roll(first, 64, 1), second)
        return carry

    lax.fori_loop(0, MMAX // 256, forward, 0)

    for i in range(ROWS):
        if i == ROWS - 1:
            block = jnp.zeros((128, 128), f32)
        else:
            block = packed[i * 128 : (i + 1) * 128, :].T
        rows[pl.ds(i, WAVES, stride=2 * ROWS), :] = block[:64]
        rows[pl.ds(ROWS + i, WAVES, stride=2 * ROWS), :] = block[64:]
    ret_ref[...] = rows[...].astype(bf16)


def cycle(scalars, weight, payload, m_row, table):
    return pl.pallas_call(
        cycle_kernel,
        in_specs=[
            pl.BlockSpec(memory_space=pltpu.SMEM),
            pl.BlockSpec(memory_space=pltpu.SMEM),
            pl.BlockSpec(memory_space=pltpu.VMEM),
            pl.BlockSpec(memory_space=pltpu.VMEM),
            pl.BlockSpec(memory_space=pltpu.VMEM),
        ],
        out_specs=[pl.BlockSpec(memory_space=pltpu.VMEM)] * 3,
        out_shape=[
            jax.ShapeDtypeStruct((128 * ROWS, 128), bf16),
            jax.ShapeDtypeStruct((3, OUTR, 384), bf16),
            jax.ShapeDtypeStruct((3, OUTR, 384), bf16),
        ],
        scratch_shapes=[
            pltpu.VMEM((128 * ROWS, 128), f32),
            pltpu.VMEM((128 * ROWS, 128), f32),
            pltpu.VMEM((576, 2 * MMAX), bf16),
            pltpu.VMEM((QUARTER // TILE, 576, TILE), bf16),
            pltpu.VMEM((3, 5264, 128), f32),
        ],
        compiler_params=params(56),
        name="cycle",
    )(scalars, weight, payload, m_row, table)


def local(spectra, legendre, block_slot, wavenumber, cycle_points, quad_weight):
    lev = lax.axis_index("lev")
    spec = jnp.transpose(spectra, (1, 0, 2))
    sent = synthesis(block_slot, spec, legendre).reshape(128, ROWS, 128)
    received = lax.all_to_all(sent, ("wave", "lev"), split_axis=0, concat_axis=0, tiled=True)
    points = lax.dynamic_slice(cycle_points, (lev,), (1,))
    weight = lax.dynamic_slice(quad_weight, (lev,), (1,))
    m_row = wavenumber.reshape(WAVES, SLOTS).T.reshape(1, MMAX)
    table = tables(points, m_row)
    scalars = jnp.concatenate([points, lev[None].astype(jnp.int32)])
    ret, keep, send = cycle(scalars, weight, received.reshape(128 * ROWS, 128), m_row, table)
    other = lax.ppermute(send, "lev", [(0, 1), (1, 0)])
    returned = lax.all_to_all(
        ret.reshape(128, ROWS, 128), ("wave", "lev"), split_axis=0, concat_axis=0, tiled=True
    )
    tendency = analysis(block_slot, returned.reshape(128 * ROWS, 128), legendre)
    own_first = lev == 0
    both = jnp.stack(
        [jnp.where(own_first, keep, other), jnp.where(own_first, other, keep)], axis=0
    )
    grid_fields = both[:, :, : HALF // 8, :].reshape(2, 3, HALF * 48)
    return (jnp.transpose(tendency, (1, 0, 2)), grid_fields)


def solution(mesh):
    placed = (P("wave", None, "lev"), P("wave", None, None), P("wave"), P(), P("wave"), P("wave"))
    return jax.shard_map(
        local,
        mesh=mesh,
        in_specs=placed,
        out_specs=(P("wave", None, "lev"), P("wave", None, "lev")),
        check_vma=False,
    )
```

```python
import functools
import math

import jax
import jax.numpy as jnp
from jax import lax
from jax.experimental import pallas as pl
from jax.experimental.pallas import tpu as pltpu
from jax.sharding import PartitionSpec as P

MMAX = 1280
NLON = 5136
NBLK = 64
WAVES = 64
SLOTS = 20
HALF = NLON // 2
PAYLOAD = 2880
ROWS = 24
QUARTER = 1296
TILE = 432
FINE = 48
COARSE = QUARTER // FINE
OUTR = 336
GROUP = 16
RUNS = ((0, 32), (32, 96), (128, 96), (224, 96), (320, 80))
STRIDE = 73

f32 = jnp.float32
bf16 = jnp.bfloat16


def params(mib):
    return pltpu.CompilerParams(vmem_limit_bytes=mib * 1024 * 1024)


def block_diagonal(block):
    zero = jnp.zeros_like(block)
    return jnp.concatenate(
        [jnp.concatenate([block, zero], axis=1), jnp.concatenate([zero, block], axis=1)], axis=0
    )


def copy_in(spec_hbm, leg_hbm, spec, leg, sems):
    copies = []
    for n, (first, count) in enumerate(RUNS):
        pair = [
            pltpu.make_async_copy(
                leg_hbm.at[pl.ds(first, count)], leg.at[pl.ds(first, count)], sems.at[0, n]
            )
        ]
        if spec is not None:
            pair.append(
                pltpu.make_async_copy(
                    spec_hbm.at[:, pl.ds(first, count)],
                    spec.at[:, pl.ds(first, count)],
                    sems.at[1, n],
                )
            )
        for copy in pair:
            copy.start()
        copies.append(pair)
    return copies


def synthesis_kernel(
    slot_ref, spec_hbm, leg_hbm, out_ref, spec, leg, sems, acc, stage, packed, rows
):
    copies = copy_in(spec_hbm, leg_hbm, spec, leg, sems)
    acc[...] = jnp.zeros_like(acc)
    packed[...] = jnp.zeros_like(packed)

    def body(g, carry):
        base = pl.multiple_of(g * GROUP, GROUP)
        for c in range(6):
            x = spec[c, pl.ds(base, GROUP), :].astype(f32)
            for t in range(12):
                stage[pl.ds(c * 12 + t, GROUP, stride=STRIDE), :] = x[:, t * 128 : (t + 1) * 128]
        for kk in range(GROUP):
            x = stage[kk * STRIDE : kk * STRIDE + 72, :].astype(bf16)
            w = block_diagonal(leg[base + kk])
            prod = jnp.dot(x, w, preferred_element_type=f32)
            slot = slot_ref[base + kk]
            acc[slot, 0:72, :] += prod[:, :128]
            acc[slot, 72:144, :] += prod[:, 128:]
        return carry

    for (first, count), pair in zip(RUNS, copies):
        for copy in pair:
            copy.wait()
        lax.fori_loop(first // GROUP, (first + count) // GROUP, body, 0)

    for q in range(SLOTS):
        for r in range(2):
            for l2 in range(2):
                packed[pl.ds((q * 2 + r) * 72 + l2, 36, stride=2), :] = acc[
                    q, l2 * 72 + r * 36 : l2 * 72 + r * 36 + 36, :
                ]
    for i in range(ROWS):
        rows[pl.ds(i, 128, stride=ROWS), :] = packed[i * 128 : (i + 1) * 128, :].T
    out_ref[...] = rows[...].astype(bf16)


def synthesis(block_slot, spec, legendre):
    return pl.pallas_call(
        synthesis_kernel,
        in_specs=[
            pl.BlockSpec(memory_space=pltpu.SMEM),
            pl.BlockSpec(memory_space=pl.ANY),
            pl.BlockSpec(memory_space=pl.ANY),
        ],
        out_specs=pl.BlockSpec(memory_space=pltpu.VMEM),
        scratch_shapes=[
            pltpu.VMEM(spec.shape, bf16),
            pltpu.VMEM(legendre.shape, bf16),
            pltpu.SemaphoreType.DMA((2, len(RUNS))),
            pltpu.VMEM((SLOTS + 1, 144, 128), f32),
            pltpu.VMEM((GROUP * 80, 128), f32),
            pltpu.VMEM((ROWS * 128, 128), f32),
            pltpu.VMEM((ROWS * 128, 128), f32),
        ],
        out_shape=jax.ShapeDtypeStruct((128 * ROWS, 128), bf16),
        compiler_params=params(60),
        name="synthesis",
    )(block_slot, spec, legendre)


def analysis_kernel(
    slot_ref, in_ref, leg_hbm, out_hbm, leg, out, in_sems, out_sems, coef, stage, packed, rows
):
    copies = copy_in(None, leg_hbm, None, leg, in_sems)
    rows[...] = in_ref[...].astype(f32)
    for i in range(ROWS - 1):
        packed[i * 128 : (i + 1) * 128, :] = rows[pl.ds(i, 128, stride=ROWS), :].T
    for q in range(SLOTS):
        for l2 in range(2):
            for r in range(2):
                stage[r * 36 : r * 36 + 36, :] = packed[
                    pl.ds((q * 2 + r) * 72 + l2, 36, stride=2), :
                ]
            coef[q, 0:72, l2 * 128 : (l2 + 1) * 128] = stage[0:72, :].astype(bf16)
    coef[SLOTS] = jnp.zeros(coef.shape[1:], bf16)

    def body(g, carry):
        base = pl.multiple_of(g * GROUP, GROUP)
        for kk in range(GROUP):
            slot = slot_ref[base + kk]
            w = block_diagonal(leg[base + kk])
            stage[kk * STRIDE : kk * STRIDE + 72, :] = lax.dot_general(
                coef[slot], w, (((1,), (1,)), ((), ())), preferred_element_type=f32
            )[:72]
        for c in range(6):
            for t in range(12):
                out[c, pl.ds(base, GROUP), t * 128 : (t + 1) * 128] = stage[
                    pl.ds(c * 12 + t, GROUP, stride=STRIDE), :
                ].astype(bf16)
        return carry

    written = []
    for n, (first, count) in enumerate(RUNS):
        copies[n][0].wait()
        lax.fori_loop(first // GROUP, (first + count) // GROUP, body, 0)
        copy = pltpu.make_async_copy(
            out.at[:, pl.ds(first, count)], out_hbm.at[:, pl.ds(first, count)], out_sems.at[n]
        )
        copy.start()
        written.append(copy)
    for copy in written:
        copy.wait()


def analysis(block_slot, payload, legendre):
    shape = (6, legendre.shape[0], 24 * NBLK)
    return pl.pallas_call(
        analysis_kernel,
        in_specs=[
            pl.BlockSpec(memory_space=pltpu.SMEM),
            pl.BlockSpec(memory_space=pltpu.VMEM),
            pl.BlockSpec(memory_space=pl.ANY),
        ],
        out_specs=pl.BlockSpec(memory_space=pl.ANY),
        scratch_shapes=[
            pltpu.VMEM(legendre.shape, bf16),
            pltpu.VMEM(shape, bf16),
            pltpu.SemaphoreType.DMA((2, len(RUNS))),
            pltpu.SemaphoreType.DMA((len(RUNS),)),
            pltpu.VMEM((SLOTS + 1, 80, 256), bf16),
            pltpu.VMEM((GROUP * 80, 128), f32),
            pltpu.VMEM((ROWS * 128, 128), f32),
            pltpu.VMEM((ROWS * 128, 128), f32),
        ],
        out_shape=jax.ShapeDtypeStruct(shape, bf16),
        compiler_params=params(60),
        name="analysis",
    )(block_slot, payload, legendre)


def cosine_sine(phase, points, inverse):
    turns = jnp.floor(phase * inverse + 0.5)
    rest = phase - turns * points
    quarter = jnp.floor(4.0 * rest * inverse + 0.5)
    z = (4.0 * rest - quarter * points) * inverse * (0.5 * math.pi)
    z2 = z * z
    s = z * (1.0 + z2 * (-1 / 6 + z2 * (1 / 120 + z2 * (-1 / 5040 + z2 * (1 / 362880)))))
    c = 1.0 + z2 * (-0.5 + z2 * (1 / 24 + z2 * (-1 / 720 + z2 * (1 / 40320))))
    odd = jnp.abs(quarter) == 1.0
    flip = jnp.abs(quarter) == 2.0
    first = jnp.where(odd, s, c)
    second = jnp.where(odd, c, s)
    cos_sign = jnp.where(flip | (quarter == 1.0), -1.0, 1.0)
    sin_sign = jnp.where(flip | (quarter == -1.0), -1.0, 1.0)
    return first * cos_sign, second * sin_sign


def table_kernel(points_ref, m_ref, out_ref, fine_c, fine_s, coarse_c, coarse_s):
    step = pl.program_id(0)
    points = jnp.full((1, MMAX), points_ref[0], jnp.int32).astype(f32)
    inverse = 1.0 / points

    @pl.when(step == 0)
    def _():
        m = m_ref[...].astype(f32)
        live = jnp.where(2.0 * m < points, 1.0, 0.0)
        for base in range(0, FINE, 8):
            index = (base + lax.broadcasted_iota(jnp.int32, (8, MMAX), 0)).astype(f32)
            c, s = cosine_sine(index * m, points, inverse)
            fine_c[base : base + 8, :] = c
            fine_s[base : base + 8, :] = s
        for base in range(0, coarse_c.shape[0], 8):
            index = (FINE * (base + lax.broadcasted_iota(jnp.int32, (8, MMAX), 0))).astype(f32)
            c, s = cosine_sine(index * m, points, inverse)
            coarse_c[base : base + 8, :] = c * live
            coarse_s[base : base + 8, :] = s * live

    each = out_ref.shape[0] // FINE
    for b in range(each):
        row = step * each + b
        for lane in range(0, MMAX, 256):
            at = slice(lane, lane + 256)
            cb = coarse_c[pl.ds(row, 1), at]
            sb = coarse_s[pl.ds(row, 1), at]
            cf = fine_c[:, at]
            sf = fine_s[:, at]
            out_ref[b * FINE : (b + 1) * FINE, at] = (cb * cf - sb * sf).astype(bf16)
            out_ref[b * FINE : (b + 1) * FINE, MMAX + lane : MMAX + lane + 256] = (
                -(sb * cf + cb * sf)
            ).astype(bf16)


def tables(points, m_row):
    each = 3 * FINE
    return pl.pallas_call(
        table_kernel,
        grid_spec=pltpu.PrefetchScalarGridSpec(
            num_scalar_prefetch=1,
            grid=(QUARTER // each,),
            in_specs=[pl.BlockSpec((1, MMAX), lambda i, s: (0, 0))],
            out_specs=pl.BlockSpec((each, 2 * MMAX), lambda i, s: (i, 0)),
            scratch_shapes=[
                pltpu.VMEM((FINE, MMAX), f32),
                pltpu.VMEM((FINE, MMAX), f32),
                pltpu.VMEM((32, MMAX), f32),
                pltpu.VMEM((32, MMAX), f32),
            ],
        ),
        out_shape=jax.ShapeDtypeStruct((QUARTER, 2 * MMAX), bf16),
        compiler_params=params(24),
        name="tables",
    )(points, m_row)


def rotation(m):
    k = m & 3
    a = jnp.where(k == 0, 1.0, jnp.where(k == 2, -1.0, 0.0))
    b = jnp.where(k == 1, 1.0, jnp.where(k == 3, -1.0, 0.0))
    sign = jnp.where((k & 1) == 0, 1.0, -1.0)
    return a.astype(f32), b.astype(f32), sign.astype(f32)


def inverse_kernel(
    scalar_ref, in_ref, m_ref, table_ref, flux, keep_ref, send_ref, rows, packed, coef, grid
):
    points = scalar_ref[0]
    lev = scalar_ref[1]
    quarter = points >> 2
    low = lax.broadcasted_iota(jnp.int32, (72, 128), 1) < 64

    rows[...] = in_ref[...].astype(f32)
    for i in range(ROWS - 1):
        block = jnp.concatenate(
            [
                rows[pl.ds(i, WAVES, stride=2 * ROWS), :],
                rows[pl.ds(ROWS + i, WAVES, stride=2 * ROWS), :],
            ],
            axis=0,
        )
        packed[i * 128 : (i + 1) * 128, :] = block.T

    for i in range(SLOTS // 2):
        lanes = slice(i * 128, (i + 1) * 128)
        m = m_ref[:, lanes]
        factor = jnp.where(m == 0, 1.0, 2.0).astype(f32)
        a, b, sign = rotation(m)
        parts = []
        for r in range(2):
            even = packed[(4 * i + r) * 72 : (4 * i + r + 1) * 72, :]
            odd = packed[(4 * i + 2 + r) * 72 : (4 * i + 3 + r) * 72, :]
            first = jnp.where(low, even, pltpu.roll(odd, 64, 1)) * factor
            second = jnp.where(low, pltpu.roll(even, 64, 1), odd) * factor
            parts.append((first, second))
        (re0, re1), (im0, im1) = parts
        for f in range(3):
            at = slice(f * 24, (f + 1) * 24)
            re = jnp.concatenate([re0[at], re1[at]], axis=0)
            im = jnp.concatenate([im0[at], im1[at]], axis=0)
            turned = [
                (re, im),
                (a * re - b * im, a * im + b * re),
                (sign * re, sign * im),
                (a * re + b * im, a * im - b * re),
            ]
            for r4 in range(4):
                out = slice(f * 192 + r4 * 48, f * 192 + (r4 + 1) * 48)
                coef[out, i * 128 : (i + 1) * 128] = turned[r4][0].astype(bf16)
                coef[out, MMAX + i * 128 : MMAX + (i + 1) * 128] = turned[r4][1].astype(bf16)

    tiles = QUARTER // TILE

    def tile(step, carry):
        start = pl.multiple_of((tiles - 1 - step) * TILE, 16)
        values = lax.dot_general(
            table_ref[pl.ds(start, TILE), :], coef[...], (((1,), (1,)), ((), ())),
            preferred_element_type=f32,
        )
        index = start + lax.broadcasted_iota(jnp.int32, (TILE, 192), 0)
        fields = [
            jnp.where(index < quarter, values[:, f * 192 : (f + 1) * 192], 0.0)
            .astype(bf16)
            .astype(f32)
            for f in range(3)
        ]
        for f in range(3):
            for r4 in range(4):
                grid[f, pl.ds(r4 * quarter + start, TILE), 0:48] = fields[f][
                    :, r4 * 48 : (r4 + 1) * 48
                ]
        products = [fields[0] * fields[2], fields[1] * fields[2], 0.5 * fields[2] * fields[2]]
        for f in range(3):
            flux[step, f * 192 : (f + 1) * 192, :] = products[f].T.astype(bf16)
        return carry

    lax.fori_loop(0, tiles, tile, 0)

    chunk = 48
    for which, ref in ((0, keep_ref), (1, send_ref)):
        half = lev if which == 0 else 1 - lev

        def place(j, carry, half=half, ref=ref):
            for f in range(3):
                pieces = []
                for s in range(8):
                    first = half * HALF + j * (8 * chunk) + s
                    piece = grid[f, pl.ds(first, chunk, stride=8), :][:, 0:48]
                    place_of = first + 8 * lax.broadcasted_iota(jnp.int32, (chunk, 48), 0)
                    pieces.append(jnp.where(place_of < points, piece, 0.0))
                ref[f, pl.ds(pl.multiple_of(j * chunk, 16), chunk), :] = jnp.concatenate(
                    pieces, axis=1
                ).astype(bf16)
            return carry

        lax.fori_loop(0, OUTR // chunk, place, 0)


def forward_kernel(weight_ref, m_ref, table_ref, flux, ret_ref, rows, packed):
    low = lax.broadcasted_iota(jnp.int32, (72, 128), 1) < 64
    tiles = QUARTER // TILE
    weight = weight_ref[0]

    def columns(n, carry):
        at = pl.multiple_of(n * 256, 256)
        cos_sum = jnp.zeros((576, 256), f32)
        sin_sum = jnp.zeros((576, 256), f32)
        for step in range(tiles):
            start = (tiles - 1 - step) * TILE
            cos_sum += jnp.dot(
                flux[step], table_ref[start : start + TILE, pl.ds(at, 256)],
                preferred_element_type=f32,
            )
            sin_sum += jnp.dot(
                flux[step], table_ref[start : start + TILE, pl.ds(at + MMAX, 256)],
                preferred_element_type=f32,
            )
        for i2 in range(2):
            lanes = slice(i2 * 128, (i2 + 1) * 128)
            a, b, sign = rotation(m_ref[:, pl.ds(at + i2 * 128, 128)])
            result = [[], []]
            for f in range(3):
                c = [cos_sum[f * 192 + r4 * 48 : f * 192 + (r4 + 1) * 48, lanes] for r4 in range(4)]
                s = [sin_sum[f * 192 + r4 * 48 : f * 192 + (r4 + 1) * 48, lanes] for r4 in range(4)]
                result[0].append(
                    (c[0] + sign * c[2] + a * (c[1] + c[3]) + b * (s[1] - s[3])) * weight
                )
                result[1].append(
                    (s[0] + sign * s[2] + a * (s[1] + s[3]) - b * (c[1] - c[3])) * weight
                )
            for r in range(2):
                first = jnp.concatenate([x[:24] for x in result[r]], axis=0)
                second = jnp.concatenate([x[24:] for x in result[r]], axis=0)
                row = pl.multiple_of((n * 8 + 4 * i2 + r) * 72, 8)
                packed[pl.ds(row, 72), :] = jnp.where(low, first, pltpu.roll(second, 64, 1))
                packed[pl.ds(row + 144, 72), :] = jnp.where(low, pltpu.roll(first, 64, 1), second)
        return carry

    lax.fori_loop(0, MMAX // 256, columns, 0)

    for i in range(ROWS):
        if i == ROWS - 1:
            block = jnp.zeros((128, 128), f32)
        else:
            block = packed[i * 128 : (i + 1) * 128, :].T
        rows[pl.ds(i, WAVES, stride=2 * ROWS), :] = block[:64]
        rows[pl.ds(ROWS + i, WAVES, stride=2 * ROWS), :] = block[64:]
    ret_ref[...] = rows[...].astype(bf16)


def inverse(scalars, payload, m_row, table):
    vmem = pl.BlockSpec(memory_space=pltpu.VMEM)
    return pl.pallas_call(
        inverse_kernel,
        in_specs=[pl.BlockSpec(memory_space=pltpu.SMEM), vmem, vmem, vmem],
        out_specs=[vmem] * 3,
        out_shape=[
            jax.ShapeDtypeStruct((QUARTER // TILE, 576, TILE), bf16),
            jax.ShapeDtypeStruct((3, OUTR, 384), bf16),
            jax.ShapeDtypeStruct((3, OUTR, 384), bf16),
        ],
        scratch_shapes=[
            pltpu.VMEM((128 * ROWS, 128), f32),
            pltpu.VMEM((128 * ROWS, 128), f32),
            pltpu.VMEM((576, 2 * MMAX), bf16),
            pltpu.VMEM((3, 5264, 128), f32),
        ],
        compiler_params=params(34),
        cost_estimate=pl.CostEstimate(
            flops=2 * QUARTER * 2 * MMAX * 576, bytes_accessed=12 << 20, transcendentals=0
        ),
        name="inverse",
    )(scalars, payload, m_row, table)


def forward(weight, m_row, table, flux):
    vmem = pl.BlockSpec(memory_space=pltpu.VMEM)
    return pl.pallas_call(
        forward_kernel,
        in_specs=[pl.BlockSpec(memory_space=pltpu.SMEM), vmem, vmem, vmem],
        out_specs=vmem,
        out_shape=jax.ShapeDtypeStruct((128 * ROWS, 128), bf16),
        scratch_shapes=[
            pltpu.VMEM((128 * ROWS, 128), f32),
            pltpu.VMEM((128 * ROWS, 128), f32),
        ],
        compiler_params=params(20),
        cost_estimate=pl.CostEstimate(
            flops=2 * QUARTER * 2 * MMAX * 576, bytes_accessed=12 << 20, transcendentals=0
        ),
        name="forward",
    )(weight, m_row, table, flux)


def local(spectra, legendre, block_slot, wavenumber, cycle_points, quad_weight):
    lev = lax.axis_index("lev")
    spec = jnp.transpose(spectra, (1, 0, 2))
    sent = synthesis(block_slot, spec, legendre).reshape(128, ROWS, 128)
    received = lax.all_to_all(sent, ("wave", "lev"), split_axis=0, concat_axis=0, tiled=True)
    points = lax.dynamic_slice(cycle_points, (lev,), (1,))
    weight = lax.dynamic_slice(quad_weight, (lev,), (1,))
    m_row = wavenumber.reshape(WAVES, SLOTS).T.reshape(1, MMAX)
    table = tables(points, m_row)
    scalars = jnp.concatenate([points, lev[None].astype(jnp.int32)])
    flux, keep, send = inverse(scalars, received.reshape(128 * ROWS, 128), m_row, table)
    other = lax.ppermute(send, "lev", [(0, 1), (1, 0)])
    ret = forward(weight, m_row, table, flux)
    returned = lax.all_to_all(
        ret.reshape(128, ROWS, 128), ("wave", "lev"), split_axis=0, concat_axis=0, tiled=True
    )
    tendency = analysis(block_slot, returned.reshape(128 * ROWS, 128), legendre)
    own_first = lev == 0
    both = jnp.stack(
        [jnp.where(own_first, keep, other), jnp.where(own_first, other, keep)], axis=0
    )
    grid_fields = both[:, :, : HALF // 8, :].reshape(2, 3, HALF * 48)
    return (jnp.transpose(tendency, (1, 0, 2)), grid_fields)


def solution(mesh):
    placed = (P("wave", None, "lev"), P("wave", None, None), P("wave"), P(), P("wave"), P("wave"))
    return jax.shard_map(
        local,
        mesh=mesh,
        in_specs=placed,
        out_specs=(P("wave", None, "lev"), P("wave", None, "lev")),
        check_vma=False,
    )
```

```python
import functools
import math

import jax
import jax.numpy as jnp
from jax import lax
from jax.experimental import pallas as pl
from jax.experimental.pallas import tpu as pltpu
from jax.sharding import PartitionSpec as P

MMAX = 1280
NLON = 5136
NBLK = 64
WAVES = 64
SLOTS = 20
HALF = NLON // 2
PAYLOAD = 2880
ROWS = 24
QUARTER = 1408
FINE = 32
CHUNK = 256
OUTR = 336
GROUP = 16
RUNS = ((0, 32), (32, 96), (128, 96), (224, 96), (320, 80))
STRIDE = 73
FEW = 5

f32 = jnp.float32
bf16 = jnp.bfloat16


def params(mib):
    return pltpu.CompilerParams(vmem_limit_bytes=mib * 1024 * 1024)


def block_diagonal(block):
    zero = jnp.zeros_like(block)
    return jnp.concatenate(
        [jnp.concatenate([block, zero], axis=1), jnp.concatenate([zero, block], axis=1)], axis=0
    )


def copy_in(spec_hbm, leg_hbm, spec, leg, sems):
    copies = []
    for n, (first, count) in enumerate(RUNS):
        pair = [
            pltpu.make_async_copy(
                leg_hbm.at[pl.ds(first, count)], leg.at[pl.ds(first, count)], sems.at[0, n]
            )
        ]
        if spec is not None:
            pair.append(
                pltpu.make_async_copy(
                    spec_hbm.at[:, pl.ds(first, count)],
                    spec.at[:, pl.ds(first, count)],
                    sems.at[1, n],
                )
            )
        for copy in pair:
            copy.start()
        copies.append(pair)
    return copies


def synthesis_kernel(
    slot_ref, spec_hbm, leg_hbm, out_ref, order_ref, count_ref,
    spec, leg, sems, acc, stage, packed, rows,
):
    copies = copy_in(spec_hbm, leg_hbm, spec, leg, sems)
    acc[...] = jnp.zeros_like(acc)
    packed[...] = jnp.zeros_like(packed)
    for q in range(SLOTS + 1):
        count_ref[q] = 0

    def body(g, carry):
        base = pl.multiple_of(g * GROUP, GROUP)
        for c in range(6):
            x = spec[c, pl.ds(base, GROUP), :].astype(f32)
            for t in range(12):
                stage[pl.ds(c * 12 + t, GROUP, stride=STRIDE), :] = x[:, t * 128 : (t + 1) * 128]

        def product(kk):
            x = stage[kk * STRIDE : kk * STRIDE + 72, :].astype(bf16)
            return jnp.dot(x, block_diagonal(leg[base + kk]), preferred_element_type=f32)

        ahead = product(0)
        for kk in range(GROUP):
            prod = ahead
            if kk < GROUP - 1:
                ahead = product(kk + 1)
            slot = slot_ref[base + kk]
            acc[slot, 0:72, :] += prod[:, :128]
            acc[slot, 72:144, :] += prod[:, 128:]
            seen = count_ref[slot]
            count_ref[slot] = seen + 1
            order_ref[slot * 20 + seen] = base + kk
        return carry

    for (first, count), pair in zip(RUNS, copies):
        for copy in pair:
            copy.wait()
        lax.fori_loop(first // GROUP, (first + count) // GROUP, body, 0, unroll=True)

    for q in range(SLOTS):
        for r in range(2):
            for l2 in range(2):
                packed[pl.ds((q * 2 + r) * 72 + l2, 36, stride=2), :] = acc[
                    q, l2 * 72 + r * 36 : l2 * 72 + r * 36 + 36, :
                ]
    for i in range(ROWS):
        rows[pl.ds(i, 128, stride=ROWS), :] = packed[i * 128 : (i + 1) * 128, :].T
    out_ref[...] = rows[...].astype(bf16)


def synthesis(block_slot, spec, legendre):
    return pl.pallas_call(
        synthesis_kernel,
        in_specs=[
            pl.BlockSpec(memory_space=pltpu.SMEM),
            pl.BlockSpec(memory_space=pltpu.HBM),
            pl.BlockSpec(memory_space=pltpu.HBM),
        ],
        out_specs=[
            pl.BlockSpec(memory_space=pltpu.VMEM),
            pl.BlockSpec(memory_space=pltpu.SMEM),
            pl.BlockSpec(memory_space=pltpu.SMEM),
        ],
        scratch_shapes=[
            pltpu.VMEM(spec.shape, bf16),
            pltpu.VMEM(legendre.shape, bf16),
            pltpu.SemaphoreType.DMA((2, len(RUNS))),
            pltpu.VMEM((SLOTS + 1, 144, 128), f32),
            pltpu.VMEM((GROUP * 80, 128), f32),
            pltpu.VMEM((ROWS * 128, 128), f32),
            pltpu.VMEM((ROWS * 128, 128), f32),
        ],
        out_shape=[
            jax.ShapeDtypeStruct((128 * ROWS, 128), bf16),
            jax.ShapeDtypeStruct((SLOTS * 20 + legendre.shape[0],), jnp.int32),
            jax.ShapeDtypeStruct((SLOTS + 1,), jnp.int32),
        ],
        compiler_params=params(60),
        name="synthesis",
    )(block_slot, spec, legendre)


def block_at(order_ref, count, before, q, i):
    free = SLOTS * 20 + q * 20 + i - before - count
    return order_ref[jnp.where(i < count, q * 20 + i, free)]


def arrange_kernel(order_ref, count_ref, leg_hbm, out_hbm, leg, out_ref, sem, out_sems):
    copy = pltpu.make_async_copy(leg_hbm, leg, sem)
    copy.start()
    copy.wait()

    def slot_body(q, before):
        count = count_ref[q]
        for g in range(5):
            for e in range(0, 4, 2):
                first = block_at(order_ref, count, before, q, g * 4 + e)
                second = block_at(order_ref, count, before, q, g * 4 + e + 1)
                pair = jnp.concatenate([leg[first], leg[second]], axis=0)
                out_ref[q * 5 + g, :, e * 64 : e * 64 + 128] = pair.T
        return before + count

    before = 0
    written = []
    for n in range(SLOTS // FEW):
        before = lax.fori_loop(n * FEW, (n + 1) * FEW, slot_body, before, unroll=FEW)
        part = pl.ds(n * FEW * 5, FEW * 5)
        copy = pltpu.make_async_copy(out_ref.at[part], out_hbm.at[part], out_sems.at[n])
        copy.start()
        written.append(copy)
    for copy in written:
        copy.wait()


def arrange(order, counts, legendre):
    smem = pl.BlockSpec(memory_space=pltpu.SMEM)
    return pl.pallas_call(
        arrange_kernel,
        in_specs=[smem, smem, pl.BlockSpec(memory_space=pltpu.HBM)],
        out_specs=pl.BlockSpec(memory_space=pltpu.HBM),
        scratch_shapes=[
            pltpu.VMEM(legendre.shape, bf16),
            pltpu.VMEM((SLOTS * 5, 128, 256), bf16),
            pltpu.SemaphoreType.DMA(()),
            pltpu.SemaphoreType.DMA((SLOTS // FEW,)),
        ],
        out_shape=jax.ShapeDtypeStruct((SLOTS * 5, 128, 256), bf16),
        compiler_params=params(60),
        cost_estimate=pl.CostEstimate(flops=1 << 32, bytes_accessed=14 << 20, transcendentals=0),
        name="arrange",
    )(order, counts, legendre)


def analysis_kernel(
    order_ref, count_ref, in_ref, leg_hbm, out_hbm,
    leg_ref, out, in_sems, out_sems, coef, stage, packed, rows,
):
    copies = []
    for n in range(SLOTS // FEW):
        part = pl.ds(n * FEW * 5, FEW * 5)
        copy = pltpu.make_async_copy(leg_hbm.at[part], leg_ref.at[part], in_sems.at[n])
        copy.start()
        copies.append(copy)
    rows[...] = in_ref[...].astype(f32)
    for i in range(ROWS - 1):
        packed[i * 128 : (i + 1) * 128, :] = rows[pl.ds(i, 128, stride=ROWS), :].T
    for q in range(SLOTS):
        for l2 in range(2):
            for r in range(2):
                stage[l2 * 72 + r * 36 : l2 * 72 + r * 36 + 36, :] = packed[
                    pl.ds((q * 2 + r) * 72 + l2, 36, stride=2), :
                ]
        coef[q] = stage[0:144, :].astype(bf16)

    low = lax.broadcasted_iota(jnp.int32, (72, 128), 1) < 64

    def slot_body(q, before):
        lhs = coef[q]
        count = count_ref[q]
        ahead = jnp.dot(lhs, leg_ref[q * 5], preferred_element_type=f32)
        for g in range(5):
            value = ahead
            if g < 4:
                ahead = jnp.dot(lhs, leg_ref[q * 5 + g + 1], preferred_element_type=f32)
            for e in range(0, 4, 2):
                first = value[:72, e * 64 : e * 64 + 128]
                second = value[72:, e * 64 : e * 64 + 128]
                even = jnp.where(low, first, pltpu.roll(second, 64, 1))
                odd = jnp.where(low, pltpu.roll(first, 64, 1), second)
                for i, part in ((g * 4 + e, even), (g * 4 + e + 1, odd)):
                    k = block_at(order_ref, count, before, q, i)
                    stage[pl.ds(pl.multiple_of(k * 72, 8), 72), :] = jnp.where(
                        i < count, part, 0.0
                    )
        return before + count

    before = 0
    for n in range(SLOTS // FEW):
        copies[n].wait()
        before = lax.fori_loop(n * FEW, (n + 1) * FEW, slot_body, before, unroll=FEW)

    def body(g, carry):
        base = pl.multiple_of(g * GROUP, GROUP)
        for c in range(6):
            for t in range(12):
                out[c, pl.ds(base, GROUP), t * 128 : (t + 1) * 128] = stage[
                    pl.ds(pl.multiple_of(base * 72, 8) + c * 12 + t, GROUP, stride=72), :
                ].astype(bf16)
        return carry

    written = []
    for n, (first, count) in enumerate(RUNS):
        lax.fori_loop(first // GROUP, (first + count) // GROUP, body, 0)
        copy = pltpu.make_async_copy(
            out.at[:, pl.ds(first, count)], out_hbm.at[:, pl.ds(first, count)], out_sems.at[n]
        )
        copy.start()
        written.append(copy)
    for copy in written:
        copy.wait()


def analysis(order, counts, payload, arranged, blocks):
    shape = (6, blocks, 24 * NBLK)
    return pl.pallas_call(
        analysis_kernel,
        in_specs=[
            pl.BlockSpec(memory_space=pltpu.SMEM),
            pl.BlockSpec(memory_space=pltpu.SMEM),
            pl.BlockSpec(memory_space=pltpu.VMEM),
            pl.BlockSpec(memory_space=pltpu.HBM),
        ],
        out_specs=pl.BlockSpec(memory_space=pltpu.HBM),
        scratch_shapes=[
            pltpu.VMEM(arranged.shape, bf16),
            pltpu.VMEM(shape, bf16),
            pltpu.SemaphoreType.DMA((SLOTS // FEW,)),
            pltpu.SemaphoreType.DMA((len(RUNS),)),
            pltpu.VMEM((SLOTS, 144, 128), bf16),
            pltpu.VMEM((blocks * 72, 128), f32),
            pltpu.VMEM((ROWS * 128, 128), f32),
            pltpu.VMEM((ROWS * 128, 128), f32),
        ],
        out_shape=jax.ShapeDtypeStruct(shape, bf16),
        compiler_params=params(48),
        name="analysis",
    )(order, counts, payload, arranged)


def cosine_sine(phase, points, inverse):
    turns = jnp.floor(phase * inverse + 0.5)
    rest = phase - turns * points
    quarter = jnp.floor(4.0 * rest * inverse + 0.5)
    z = (4.0 * rest - quarter * points) * inverse * (0.5 * math.pi)
    z2 = z * z
    s = z * (1.0 + z2 * (-1 / 6 + z2 * (1 / 120 + z2 * (-1 / 5040 + z2 * (1 / 362880)))))
    c = 1.0 + z2 * (-0.5 + z2 * (1 / 24 + z2 * (-1 / 720 + z2 * (1 / 40320))))
    odd = jnp.abs(quarter) == 1.0
    flip = jnp.abs(quarter) == 2.0
    first = jnp.where(odd, s, c)
    second = jnp.where(odd, c, s)
    cos_sign = jnp.where(flip | (quarter == 1.0), -1.0, 1.0)
    sin_sign = jnp.where(flip | (quarter == -1.0), -1.0, 1.0)
    return first * cos_sign, second * sin_sign


def table_kernel(
    points_ref, m_ref, out_hbm, flip_hbm,
    out_ref, flip_ref, sems, fine_c, fine_s, coarse_c, coarse_s, column, turn_c, turn_s,
):
    count = points_ref[lax.axis_index("lev")]
    points = jnp.full((1, MMAX), count, jnp.int32).astype(f32)
    inverse = 1.0 / points
    m = m_ref[...].astype(f32)
    live = jnp.where(2.0 * m < points, 1.0, 0.0)
    for base in range(0, FINE, 8):
        index = (base + lax.broadcasted_iota(jnp.int32, (8, MMAX), 0)).astype(f32)
        c, s = cosine_sine(index * m, points, inverse)
        fine_c[base : base + 8, :] = c
        fine_s[base : base + 8, :] = s
    for base in range(0, coarse_c.shape[0], 8):
        index = (FINE * (base + lax.broadcasted_iota(jnp.int32, (8, MMAX), 0))).astype(f32)
        c, s = cosine_sine(index * m, points, inverse)
        coarse_c[base : base + 8, :] = c * live
        coarse_s[base : base + 8, :] = s * live

    def row_body(row, carry):
        rows = pl.ds(pl.multiple_of(row * FINE, FINE), FINE)
        for n in range(MMAX // CHUNK):
            at = slice(n * CHUNK, (n + 1) * CHUNK)
            cb = coarse_c[pl.ds(row, 1), at]
            sb = coarse_s[pl.ds(row, 1), at]
            cf = fine_c[:, at]
            sf = fine_s[:, at]
            out_ref[n, 0, rows, :] = (cb * cf - sb * sf).astype(bf16)
            out_ref[n, 1, rows, :] = (-(sb * cf + cb * sf)).astype(bf16)
        return carry

    written = []

    def write(source, target, n):
        copy = pltpu.make_async_copy(source, target, sems.at[n])
        copy.start()
        written.append(copy)

    few = QUARTER // FINE // 4
    for n in range(4):
        lax.fori_loop(n * few, (n + 1) * few, row_body, 0)
        part = pl.ds(n * few * FINE, few * FINE)
        write(out_ref.at[:, :, part], out_hbm.at[:, :, part], n)

    whole_c, whole_s = cosine_sine(128.0 * m, points, inverse)
    for n in range(MMAX // 128):
        at = slice(n * 128, (n + 1) * 128)
        for row, target in ((m, column), (whole_c, turn_c), (whole_s, turn_s)):
            target[at, :] = jnp.broadcast_to(row[:, at], (128, 128)).T
    points_row = points[:, :128]
    inverse_row = inverse[:, :128]
    lane = lax.broadcasted_iota(jnp.int32, (32, 128), 1).astype(f32)

    def column_body(g, carry):
        at = pl.multiple_of(g * 32, 32)
        mc = column[pl.ds(at, 32), :]
        alive = jnp.where(2.0 * mc < points_row, 1.0, 0.0)
        c, s = cosine_sine(lane * mc, points_row, inverse_row)
        c, s = c * alive, s * alive
        tc, ts = turn_c[pl.ds(at, 32), :], turn_s[pl.ds(at, 32), :]
        for a in range(QUARTER // 128):
            flip_ref[pl.ds(at, 32), a * 128 : (a + 1) * 128] = c.astype(bf16)
            flip_ref[pl.ds(MMAX + at, 32), a * 128 : (a + 1) * 128] = (-s).astype(bf16)
            c, s = c * tc - s * ts, s * tc + c * ts
        return carry

    for n in range(4):
        lax.fori_loop(n * 10, (n + 1) * 10, column_body, 0, unroll=2)
        for r in range(2):
            part = pl.ds(r * MMAX + n * 320, 320)
            write(flip_ref.at[part], flip_hbm.at[part], 4 + 2 * n + r)
    for copy in written:
        copy.wait()


def tables(points, m_row):
    vmem = pl.BlockSpec(memory_space=pltpu.VMEM)
    return pl.pallas_call(
        table_kernel,
        in_specs=[pl.BlockSpec(memory_space=pltpu.SMEM), vmem],
        out_specs=[pl.BlockSpec(memory_space=pltpu.HBM)] * 2,
        scratch_shapes=[
            pltpu.VMEM((MMAX // CHUNK, 2, QUARTER, CHUNK), bf16),
            pltpu.VMEM((2 * MMAX, QUARTER), bf16),
            pltpu.SemaphoreType.DMA((12,)),
            pltpu.VMEM((FINE, MMAX), f32),
            pltpu.VMEM((FINE, MMAX), f32),
            pltpu.VMEM((48, MMAX), f32),
            pltpu.VMEM((48, MMAX), f32),
            pltpu.VMEM((MMAX, 128), f32),
            pltpu.VMEM((MMAX, 128), f32),
            pltpu.VMEM((MMAX, 128), f32),
        ],
        out_shape=[
            jax.ShapeDtypeStruct((MMAX // CHUNK, 2, QUARTER, CHUNK), bf16),
            jax.ShapeDtypeStruct((2 * MMAX, QUARTER), bf16),
        ],
        compiler_params=params(60),
        name="tables",
    )(points, m_row)


def rotation(m):
    k = m & 3
    a = jnp.where(k == 0, 1.0, jnp.where(k == 2, -1.0, 0.0))
    b = jnp.where(k == 1, 1.0, jnp.where(k == 3, -1.0, 0.0))
    sign = jnp.where((k & 1) == 0, 1.0, -1.0)
    return a.astype(f32), b.astype(f32), sign.astype(f32)


def unpack_kernel(in_ref, m_ref, coef, rows, packed):
    low = lax.broadcasted_iota(jnp.int32, (72, 128), 1) < 64

    rows[...] = in_ref[...].astype(f32)
    for i in range(ROWS - 1):
        block = jnp.concatenate(
            [
                rows[pl.ds(i, WAVES, stride=2 * ROWS), :],
                rows[pl.ds(ROWS + i, WAVES, stride=2 * ROWS), :],
            ],
            axis=0,
        )
        packed[i * 128 : (i + 1) * 128, :] = block.T

    for i in range(SLOTS // 2):
        lanes = slice(i * 128, (i + 1) * 128)
        m = m_ref[:, lanes]
        factor = jnp.where(m == 0, 1.0, 2.0).astype(f32)
        a, b, sign = rotation(m)
        parts = []
        for r in range(2):
            even = packed[(4 * i + r) * 72 : (4 * i + r + 1) * 72, :]
            odd = packed[(4 * i + 2 + r) * 72 : (4 * i + 3 + r) * 72, :]
            first = jnp.where(low, even, pltpu.roll(odd, 64, 1)) * factor
            second = jnp.where(low, pltpu.roll(even, 64, 1), odd) * factor
            parts.append((first, second))
        (re0, re1), (im0, im1) = parts
        for f in range(3):
            at = slice(f * 24, (f + 1) * 24)
            re = jnp.concatenate([re0[at], re1[at]], axis=0)
            im = jnp.concatenate([im0[at], im1[at]], axis=0)
            turned = [
                (re, im),
                (a * re - b * im, a * im + b * re),
                (sign * re, sign * im),
                (a * re + b * im, a * im - b * re),
            ]
            for r4 in range(4):
                out = slice(f * 192 + r4 * 48, f * 192 + (r4 + 1) * 48)
                coef[out, i * 128 : (i + 1) * 128] = turned[r4][0].astype(bf16)
                coef[out, MMAX + i * 128 : MMAX + (i + 1) * 128] = turned[r4][1].astype(bf16)


def inverse_kernel(points_ref, coef, flip, flux, keep_ref, send_ref, grid):
    lev = lax.axis_index("lev")
    points = points_ref[lev]
    quarter = points >> 2

    def transform(start, size):
        values = jnp.dot(
            coef[...], flip[:, pl.ds(start, size)], preferred_element_type=f32
        )
        index = start + lax.broadcasted_iota(jnp.int32, (192, size), 1)
        fields = [
            jnp.where(index < quarter, values[f * 192 : (f + 1) * 192], 0.0)
            .astype(bf16)
            .astype(f32)
            for f in range(3)
        ]
        products = [fields[0] * fields[2], fields[1] * fields[2], 0.5 * fields[2] * fields[2]]
        for f in range(3):
            flux[f * 192 : (f + 1) * 192, pl.ds(start, size)] = products[f].astype(bf16)
        for f in range(3):
            for r4 in range(4):
                grid[f, pl.ds(r4 * quarter + start, size), 0:48] = fields[f][
                    r4 * 48 : (r4 + 1) * 48
                ].T

    transform(QUARTER - 128, 128)

    def tile(step, carry):
        transform(pl.multiple_of((QUARTER // CHUNK - 1 - step) * CHUNK, CHUNK), CHUNK)
        return carry

    lax.fori_loop(0, QUARTER // CHUNK, tile, 0, unroll=5)

    chunk = 48
    for which, ref in ((0, keep_ref), (1, send_ref)):
        half = lev if which == 0 else 1 - lev

        def place(j, carry, half=half, ref=ref):
            lines = []
            for f in range(3):
                pieces = []
                for s in range(8):
                    first = half * HALF + j * (8 * chunk) + s
                    piece = grid[f, pl.ds(first, chunk, stride=8), :][:, 0:48]
                    place_of = first + 8 * lax.broadcasted_iota(jnp.int32, (chunk, 48), 0)
                    pieces.append(jnp.where(place_of < points, piece, 0.0))
                lines.append(jnp.concatenate(pieces, axis=1).astype(bf16))
            for f in range(3):
                ref[f, pl.ds(pl.multiple_of(j * chunk, 16), chunk), :] = lines[f]
            return carry

        lax.fori_loop(0, OUTR // chunk, place, 0, unroll=7)


def forward_kernel(weight_ref, m_ref, table, flux, ret_ref, rows, packed):
    low = lax.broadcasted_iota(jnp.int32, (72, 128), 1) < 64
    weight = weight_ref[lax.axis_index("lev")]

    for n in range(MMAX // CHUNK):
        at = n * CHUNK
        cos_sum = jnp.dot(flux[...], table[n, 0], preferred_element_type=f32)
        sin_sum = jnp.dot(flux[...], table[n, 1], preferred_element_type=f32)
        for i2 in range(2):
            lanes = slice(i2 * 128, (i2 + 1) * 128)
            a, b, sign = rotation(m_ref[:, pl.ds(at + i2 * 128, 128)])
            result = [[], []]
            for f in range(3):
                c = [cos_sum[f * 192 + r4 * 48 : f * 192 + (r4 + 1) * 48, lanes] for r4 in range(4)]
                s = [sin_sum[f * 192 + r4 * 48 : f * 192 + (r4 + 1) * 48, lanes] for r4 in range(4)]
                result[0].append(
                    (c[0] + sign * c[2] + a * (c[1] + c[3]) + b * (s[1] - s[3])) * weight
                )
                result[1].append(
                    (s[0] + sign * s[2] + a * (s[1] + s[3]) - b * (c[1] - c[3])) * weight
                )
            for r in range(2):
                first = jnp.concatenate([x[:24] for x in result[r]], axis=0)
                second = jnp.concatenate([x[24:] for x in result[r]], axis=0)
                row = (n * 8 + 4 * i2 + r) * 72
                packed[pl.ds(row, 72), :] = jnp.where(low, first, pltpu.roll(second, 64, 1))
                packed[pl.ds(row + 144, 72), :] = jnp.where(low, pltpu.roll(first, 64, 1), second)

    for i in range(ROWS):
        if i == ROWS - 1:
            block = jnp.zeros((128, 128), f32)
        else:
            block = packed[i * 128 : (i + 1) * 128, :].T
        rows[pl.ds(i, WAVES, stride=2 * ROWS), :] = block[:64]
        rows[pl.ds(ROWS + i, WAVES, stride=2 * ROWS), :] = block[64:]
    ret_ref[...] = rows[...].astype(bf16)


def unpack(payload, m_row):
    vmem = pl.BlockSpec(memory_space=pltpu.VMEM)
    return pl.pallas_call(
        unpack_kernel,
        in_specs=[vmem, vmem],
        out_specs=vmem,
        out_shape=jax.ShapeDtypeStruct((576, 2 * MMAX), bf16),
        scratch_shapes=[
            pltpu.VMEM((128 * ROWS, 128), f32),
            pltpu.VMEM((128 * ROWS, 128), f32),
        ],
        compiler_params=params(16),
        cost_estimate=pl.CostEstimate(flops=1 << 33, bytes_accessed=1 << 20, transcendentals=0),
        name="unpack",
    )(payload, m_row)


def inverse(points, coef, flip):
    vmem = pl.BlockSpec(memory_space=pltpu.VMEM)
    return pl.pallas_call(
        inverse_kernel,
        in_specs=[pl.BlockSpec(memory_space=pltpu.SMEM), vmem, vmem],
        out_specs=[vmem] * 3,
        out_shape=[
            jax.ShapeDtypeStruct((576, QUARTER), bf16),
            jax.ShapeDtypeStruct((3, OUTR, 384), bf16),
            jax.ShapeDtypeStruct((3, OUTR, 384), bf16),
        ],
        scratch_shapes=[pltpu.VMEM((3, 5264, 128), f32)],
        compiler_params=params(20),
        cost_estimate=pl.CostEstimate(
            flops=2 * QUARTER * 2 * MMAX * 576, bytes_accessed=12 << 20, transcendentals=0
        ),
        name="inverse",
    )(points, coef, flip)


def forward(weight, m_row, table, flux):
    vmem = pl.BlockSpec(memory_space=pltpu.VMEM)
    return pl.pallas_call(
        forward_kernel,
        in_specs=[
            pl.BlockSpec(memory_space=pltpu.SMEM), vmem, vmem, vmem
        ],
        out_specs=vmem,
        out_shape=jax.ShapeDtypeStruct((128 * ROWS, 128), bf16),
        scratch_shapes=[
            pltpu.VMEM((128 * ROWS, 128), f32),
            pltpu.VMEM((128 * ROWS, 128), f32),
        ],
        compiler_params=params(20),
        cost_estimate=pl.CostEstimate(
            flops=2 * QUARTER * 2 * MMAX * 576, bytes_accessed=12 << 20, transcendentals=0
        ),
        name="forward",
    )(weight, m_row, table, flux)


def local(spectra, legendre, block_slot, wavenumber, cycle_points, quad_weight):
    lev = lax.axis_index("lev")
    spec = jnp.transpose(spectra, (1, 0, 2))
    sent, order, counts = synthesis(block_slot, spec, legendre)
    sent = sent.reshape(128, ROWS, 128)
    received = lax.all_to_all(sent, ("wave", "lev"), split_axis=0, concat_axis=0, tiled=True)
    m_row = wavenumber.reshape(WAVES, SLOTS).T.reshape(1, MMAX)
    table, flip = tables(cycle_points, m_row)
    coef = unpack(received.reshape(128 * ROWS, 128), m_row)
    flux, keep, send = inverse(cycle_points, coef, flip)
    other = lax.ppermute(send, "lev", [(0, 1), (1, 0)])
    ret = forward(quad_weight, m_row, table, flux)
    returned = lax.all_to_all(
        ret.reshape(128, ROWS, 128), ("wave", "lev"), split_axis=0, concat_axis=0, tiled=True
    )
    arranged = arrange(order, counts, legendre)
    tendency = analysis(
        order, counts, returned.reshape(128 * ROWS, 128), arranged, legendre.shape[0]
    )
    own_first = lev == 0
    both = jnp.stack(
        [jnp.where(own_first, keep, other), jnp.where(own_first, other, keep)], axis=0
    )
    grid_fields = both[:, :, : HALF // 8, :].reshape(2, 3, HALF * 48)
    return (jnp.transpose(tendency, (1, 0, 2)), grid_fields)


def solution(mesh):
    placed = (P("wave", None, "lev"), P("wave", None, None), P("wave"), P(), P("wave"), P("wave"))
    return jax.shard_map(
        local,
        mesh=mesh,
        in_specs=placed,
        out_specs=(P("wave", None, "lev"), P("wave", None, "lev")),
        check_vma=False,
    )
```

```python
import functools
import math

import jax
import jax.numpy as jnp
from jax import lax
from jax.experimental import pallas as pl
from jax.experimental.pallas import tpu as pltpu
from jax.sharding import PartitionSpec as P

MMAX = 1280
NLON = 5136
NBLK = 64
WAVES = 64
SLOTS = 20
HALF = NLON // 2
PAYLOAD = 2880
ROWS = 24
QUARTER = 1408
FINE = 32
CHUNK = 256
OUTR = 336
GROUP = 16
RUNS = ((0, 32), (32, 96), (128, 96), (224, 96), (320, 80))
ARRIVALS = ((0, 16), (16, 64), (80, 96), (176, 112), (288, 112))
STRIDE = 73
FEW = 5

f32 = jnp.float32
bf16 = jnp.bfloat16


def params(mib):
    return pltpu.CompilerParams(vmem_limit_bytes=mib * 1024 * 1024)


def block_diagonal(block):
    zero = jnp.zeros_like(block)
    return jnp.concatenate(
        [jnp.concatenate([block, zero], axis=1), jnp.concatenate([zero, block], axis=1)], axis=0
    )


def copy_in(spec_hbm, leg_hbm, spec, leg, sems):
    copies = []
    for n, (first, count) in enumerate(ARRIVALS):
        pair = [
            pltpu.make_async_copy(
                leg_hbm.at[pl.ds(first, count)], leg.at[pl.ds(first, count)], sems.at[0, n]
            )
        ]
        if spec is not None:
            pair.append(
                pltpu.make_async_copy(
                    spec_hbm.at[:, pl.ds(first, count)],
                    spec.at[:, pl.ds(first, count)],
                    sems.at[1, n],
                )
            )
        for copy in pair:
            copy.start()
        copies.append(pair)
    return copies


def synthesis_kernel(
    slot_ref, spec_hbm, leg_hbm, out_ref, order_ref, count_ref,
    spec, leg, sems, acc, stage, packed, rows,
):
    copies = copy_in(spec_hbm, leg_hbm, spec, leg, sems)
    acc[...] = jnp.zeros_like(acc)
    packed[...] = jnp.zeros_like(packed)
    for q in range(SLOTS + 1):
        count_ref[q] = 0

    def body(g, carry):
        base = pl.multiple_of(g * GROUP, GROUP)
        for c in range(6):
            x = spec[c, pl.ds(base, GROUP), :].astype(f32)
            for t in range(12):
                stage[pl.ds(c * 12 + t, GROUP, stride=STRIDE), :] = x[:, t * 128 : (t + 1) * 128]

        def product(kk):
            x = stage[kk * STRIDE : kk * STRIDE + 72, :].astype(bf16)
            return jnp.dot(x, block_diagonal(leg[base + kk]), preferred_element_type=f32)

        ahead = product(0)
        for kk in range(GROUP):
            prod = ahead
            if kk < GROUP - 1:
                ahead = product(kk + 1)
            slot = slot_ref[base + kk]
            acc[slot, 0:72, :] += prod[:, :128]
            acc[slot, 72:144, :] += prod[:, 128:]
            seen = count_ref[slot]
            count_ref[slot] = seen + 1
            order_ref[slot * 20 + seen] = base + kk
        return carry

    for (first, count), pair in zip(ARRIVALS, copies):
        for copy in pair:
            copy.wait()
        lax.fori_loop(first // GROUP, (first + count) // GROUP, body, 0, unroll=True)

    for q in range(SLOTS):
        for r in range(2):
            for l2 in range(2):
                packed[pl.ds((q * 2 + r) * 72 + l2, 36, stride=2), :] = acc[
                    q, l2 * 72 + r * 36 : l2 * 72 + r * 36 + 36, :
                ]
    for i in range(ROWS):
        rows[pl.ds(i, 128, stride=ROWS), :] = packed[i * 128 : (i + 1) * 128, :].T
    out_ref[...] = rows[...].astype(bf16)


def synthesis(block_slot, spec, legendre):
    return pl.pallas_call(
        synthesis_kernel,
        in_specs=[
            pl.BlockSpec(memory_space=pltpu.SMEM),
            pl.BlockSpec(memory_space=pltpu.HBM),
            pl.BlockSpec(memory_space=pltpu.HBM),
        ],
        out_specs=[
            pl.BlockSpec(memory_space=pltpu.VMEM),
            pl.BlockSpec(memory_space=pltpu.SMEM),
            pl.BlockSpec(memory_space=pltpu.SMEM),
        ],
        scratch_shapes=[
            pltpu.VMEM(spec.shape, bf16),
            pltpu.VMEM(legendre.shape, bf16),
            pltpu.SemaphoreType.DMA((2, len(ARRIVALS))),
            pltpu.VMEM((SLOTS + 1, 144, 128), f32),
            pltpu.VMEM((GROUP * 80, 128), f32),
            pltpu.VMEM((ROWS * 128, 128), f32),
            pltpu.VMEM((ROWS * 128, 128), f32),
        ],
        out_shape=[
            jax.ShapeDtypeStruct((128 * ROWS, 128), bf16),
            jax.ShapeDtypeStruct((SLOTS * 20 + legendre.shape[0],), jnp.int32),
            jax.ShapeDtypeStruct((SLOTS + 1,), jnp.int32),
        ],
        compiler_params=params(60),
        name="synthesis",
    )(block_slot, spec, legendre)


def block_at(order_ref, count, before, q, i):
    free = SLOTS * 20 + q * 20 + i - before - count
    return order_ref[jnp.where(i < count, q * 20 + i, free)]


def arrange_kernel(order_ref, count_ref, leg_hbm, out_hbm, leg, out_ref, sem, out_sems):
    copy = pltpu.make_async_copy(leg_hbm, leg, sem)
    copy.start()
    copy.wait()

    def slot_body(q, before):
        count = count_ref[q]
        for g in range(5):
            for e in range(0, 4, 2):
                first = block_at(order_ref, count, before, q, g * 4 + e)
                second = block_at(order_ref, count, before, q, g * 4 + e + 1)
                pair = jnp.concatenate([leg[first], leg[second]], axis=0)
                out_ref[q * 5 + g, :, e * 64 : e * 64 + 128] = pair.T
        return before + count

    before = 0
    written = []
    for n in range(SLOTS // FEW):
        before = lax.fori_loop(n * FEW, (n + 1) * FEW, slot_body, before, unroll=FEW)
        part = pl.ds(n * FEW * 5, FEW * 5)
        copy = pltpu.make_async_copy(out_ref.at[part], out_hbm.at[part], out_sems.at[n])
        copy.start()
        written.append(copy)
    for copy in written:
        copy.wait()


def arrange(order, counts, legendre):
    smem = pl.BlockSpec(memory_space=pltpu.SMEM)
    return pl.pallas_call(
        arrange_kernel,
        in_specs=[smem, smem, pl.BlockSpec(memory_space=pltpu.HBM)],
        out_specs=pl.BlockSpec(memory_space=pltpu.HBM),
        scratch_shapes=[
            pltpu.VMEM(legendre.shape, bf16),
            pltpu.VMEM((SLOTS * 5, 128, 256), bf16),
            pltpu.SemaphoreType.DMA(()),
            pltpu.SemaphoreType.DMA((SLOTS // FEW,)),
        ],
        out_shape=jax.ShapeDtypeStruct((SLOTS * 5, 128, 256), bf16),
        compiler_params=params(60),
        cost_estimate=pl.CostEstimate(flops=1 << 32, bytes_accessed=14 << 20, transcendentals=0),
        name="arrange",
    )(order, counts, legendre)


def analysis_kernel(
    order_ref, count_ref, in_ref, leg_hbm, out_hbm,
    leg_ref, out, in_sems, out_sems, coef, stage, packed, rows,
):
    copies = []
    for n in range(SLOTS // FEW):
        part = pl.ds(n * FEW * 5, FEW * 5)
        copy = pltpu.make_async_copy(leg_hbm.at[part], leg_ref.at[part], in_sems.at[n])
        copy.start()
        copies.append(copy)
    rows[...] = in_ref[...].astype(f32)
    for i in range(ROWS - 1):
        packed[i * 128 : (i + 1) * 128, :] = rows[pl.ds(i, 128, stride=ROWS), :].T
    for q in range(SLOTS):
        for l2 in range(2):
            for r in range(2):
                stage[l2 * 72 + r * 36 : l2 * 72 + r * 36 + 36, :] = packed[
                    pl.ds((q * 2 + r) * 72 + l2, 36, stride=2), :
                ]
        coef[q] = stage[0:144, :].astype(bf16)

    low = lax.broadcasted_iota(jnp.int32, (72, 128), 1) < 64

    def slot_body(q, before):
        lhs = coef[q]
        count = count_ref[q]
        ahead = jnp.dot(lhs, leg_ref[q * 5], preferred_element_type=f32)
        for g in range(5):
            value = ahead
            if g < 4:
                ahead = jnp.dot(lhs, leg_ref[q * 5 + g + 1], preferred_element_type=f32)
            for e in range(0, 4, 2):
                first = value[:72, e * 64 : e * 64 + 128]
                second = value[72:, e * 64 : e * 64 + 128]
                even = jnp.where(low, first, pltpu.roll(second, 64, 1))
                odd = jnp.where(low, pltpu.roll(first, 64, 1), second)
                for i, part in ((g * 4 + e, even), (g * 4 + e + 1, odd)):
                    k = block_at(order_ref, count, before, q, i)
                    stage[pl.ds(pl.multiple_of(k * 72, 8), 72), :] = jnp.where(
                        i < count, part, 0.0
                    )
        return before + count

    before = 0
    for n in range(SLOTS // FEW):
        copies[n].wait()
        before = lax.fori_loop(n * FEW, (n + 1) * FEW, slot_body, before, unroll=FEW)

    def body(g, carry):
        base = pl.multiple_of(g * GROUP, GROUP)
        for c in range(6):
            for t in range(12):
                out[c, pl.ds(base, GROUP), t * 128 : (t + 1) * 128] = stage[
                    pl.ds(pl.multiple_of(base * 72, 8) + c * 12 + t, GROUP, stride=72), :
                ].astype(bf16)
        return carry

    written = []
    for n, (first, count) in enumerate(RUNS):
        lax.fori_loop(first // GROUP, (first + count) // GROUP, body, 0)
        copy = pltpu.make_async_copy(
            out.at[:, pl.ds(first, count)], out_hbm.at[:, pl.ds(first, count)], out_sems.at[n]
        )
        copy.start()
        written.append(copy)
    for copy in written:
        copy.wait()


def analysis(order, counts, payload, arranged, blocks):
    shape = (6, blocks, 24 * NBLK)
    return pl.pallas_call(
        analysis_kernel,
        in_specs=[
            pl.BlockSpec(memory_space=pltpu.SMEM),
            pl.BlockSpec(memory_space=pltpu.SMEM),
            pl.BlockSpec(memory_space=pltpu.VMEM),
            pl.BlockSpec(memory_space=pltpu.HBM),
        ],
        out_specs=pl.BlockSpec(memory_space=pltpu.HBM),
        scratch_shapes=[
            pltpu.VMEM(arranged.shape, bf16),
            pltpu.VMEM(shape, bf16),
            pltpu.SemaphoreType.DMA((SLOTS // FEW,)),
            pltpu.SemaphoreType.DMA((len(RUNS),)),
            pltpu.VMEM((SLOTS, 144, 128), bf16),
            pltpu.VMEM((blocks * 72, 128), f32),
            pltpu.VMEM((ROWS * 128, 128), f32),
            pltpu.VMEM((ROWS * 128, 128), f32),
        ],
        out_shape=jax.ShapeDtypeStruct(shape, bf16),
        compiler_params=params(48),
        name="analysis",
    )(order, counts, payload, arranged)


def cosine_sine(phase, points, inverse):
    turns = jnp.floor(phase * inverse + 0.5)
    rest = phase - turns * points
    quarter = jnp.floor(4.0 * rest * inverse + 0.5)
    z = (4.0 * rest - quarter * points) * inverse * (0.5 * math.pi)
    z2 = z * z
    s = z * (1.0 + z2 * (-1 / 6 + z2 * (1 / 120 + z2 * (-1 / 5040 + z2 * (1 / 362880)))))
    c = 1.0 + z2 * (-0.5 + z2 * (1 / 24 + z2 * (-1 / 720 + z2 * (1 / 40320))))
    odd = jnp.abs(quarter) == 1.0
    flip = jnp.abs(quarter) == 2.0
    first = jnp.where(odd, s, c)
    second = jnp.where(odd, c, s)
    cos_sign = jnp.where(flip | (quarter == 1.0), -1.0, 1.0)
    sin_sign = jnp.where(flip | (quarter == -1.0), -1.0, 1.0)
    return first * cos_sign, second * sin_sign


def table_kernel(
    points_ref, m_ref, out_hbm, flip_hbm,
    out_ref, flip_ref, sems, fine_c, fine_s, coarse_c, coarse_s, column, turn_c, turn_s,
):
    count = points_ref[lax.axis_index("lev")]
    points = jnp.full((1, MMAX), count, jnp.int32).astype(f32)
    inverse = 1.0 / points
    m = m_ref[...].astype(f32)
    live = jnp.where(2.0 * m < points, 1.0, 0.0)
    for base in range(0, FINE, 8):
        index = (base + lax.broadcasted_iota(jnp.int32, (8, MMAX), 0)).astype(f32)
        c, s = cosine_sine(index * m, points, inverse)
        fine_c[base : base + 8, :] = c
        fine_s[base : base + 8, :] = s
    for base in range(0, coarse_c.shape[0], 8):
        index = (FINE * (base + lax.broadcasted_iota(jnp.int32, (8, MMAX), 0))).astype(f32)
        c, s = cosine_sine(index * m, points, inverse)
        coarse_c[base : base + 8, :] = c * live
        coarse_s[base : base + 8, :] = s * live

    def row_body(row, carry):
        rows = pl.ds(pl.multiple_of(row * FINE, FINE), FINE)
        for n in range(MMAX // CHUNK):
            at = slice(n * CHUNK, (n + 1) * CHUNK)
            cb = coarse_c[pl.ds(row, 1), at]
            sb = coarse_s[pl.ds(row, 1), at]
            cf = fine_c[:, at]
            sf = fine_s[:, at]
            out_ref[n, 0, rows, :] = (cb * cf - sb * sf).astype(bf16)
            out_ref[n, 1, rows, :] = (-(sb * cf + cb * sf)).astype(bf16)
        return carry

    written = []

    def write(source, target, n):
        copy = pltpu.make_async_copy(source, target, sems.at[n])
        copy.start()
        written.append(copy)

    few = QUARTER // FINE // 4
    for n in range(4):
        lax.fori_loop(n * few, (n + 1) * few, row_body, 0)
        part = pl.ds(n * few * FINE, few * FINE)
        write(out_ref.at[:, :, part], out_hbm.at[:, :, part], n)

    whole_c, whole_s = cosine_sine(128.0 * m, points, inverse)
    for n in range(MMAX // 128):
        at = slice(n * 128, (n + 1) * 128)
        for row, target in ((m, column), (whole_c, turn_c), (whole_s, turn_s)):
            target[at, :] = jnp.broadcast_to(row[:, at], (128, 128)).T
    points_row = points[:, :128]
    inverse_row = inverse[:, :128]
    lane = lax.broadcasted_iota(jnp.int32, (32, 128), 1).astype(f32)

    def column_body(g, carry):
        at = pl.multiple_of(g * 32, 32)
        mc = column[pl.ds(at, 32), :]
        alive = jnp.where(2.0 * mc < points_row, 1.0, 0.0)
        c, s = cosine_sine(lane * mc, points_row, inverse_row)
        c, s = c * alive, s * alive
        tc, ts = turn_c[pl.ds(at, 32), :], turn_s[pl.ds(at, 32), :]
        for a in range(QUARTER // 128):
            flip_ref[pl.ds(at, 32), a * 128 : (a + 1) * 128] = c.astype(bf16)
            flip_ref[pl.ds(MMAX + at, 32), a * 128 : (a + 1) * 128] = (-s).astype(bf16)
            c, s = c * tc - s * ts, s * tc + c * ts
        return carry

    for n in range(4):
        lax.fori_loop(n * 10, (n + 1) * 10, column_body, 0, unroll=2)
        for r in range(2):
            part = pl.ds(r * MMAX + n * 320, 320)
            write(flip_ref.at[part], flip_hbm.at[part], 4 + 2 * n + r)
    for copy in written:
        copy.wait()


def tables(points, m_row):
    vmem = pl.BlockSpec(memory_space=pltpu.VMEM)
    return pl.pallas_call(
        table_kernel,
        in_specs=[pl.BlockSpec(memory_space=pltpu.SMEM), vmem],
        out_specs=[pl.BlockSpec(memory_space=pltpu.HBM)] * 2,
        scratch_shapes=[
            pltpu.VMEM((MMAX // CHUNK, 2, QUARTER, CHUNK), bf16),
            pltpu.VMEM((2 * MMAX, QUARTER), bf16),
            pltpu.SemaphoreType.DMA((12,)),
            pltpu.VMEM((FINE, MMAX), f32),
            pltpu.VMEM((FINE, MMAX), f32),
            pltpu.VMEM((48, MMAX), f32),
            pltpu.VMEM((48, MMAX), f32),
            pltpu.VMEM((MMAX, 128), f32),
            pltpu.VMEM((MMAX, 128), f32),
            pltpu.VMEM((MMAX, 128), f32),
        ],
        out_shape=[
            jax.ShapeDtypeStruct((MMAX // CHUNK, 2, QUARTER, CHUNK), bf16),
            jax.ShapeDtypeStruct((2 * MMAX, QUARTER), bf16),
        ],
        compiler_params=params(60),
        name="tables",
    )(points, m_row)


def rotation(m):
    k = m & 3
    a = jnp.where(k == 0, 1.0, jnp.where(k == 2, -1.0, 0.0))
    b = jnp.where(k == 1, 1.0, jnp.where(k == 3, -1.0, 0.0))
    sign = jnp.where((k & 1) == 0, 1.0, -1.0)
    return a.astype(f32), b.astype(f32), sign.astype(f32)


def unpack_kernel(in_ref, m_ref, coef, rows, packed):
    low = lax.broadcasted_iota(jnp.int32, (72, 128), 1) < 64

    rows[...] = in_ref[...].astype(f32)
    for i in range(ROWS - 1):
        block = jnp.concatenate(
            [
                rows[pl.ds(i, WAVES, stride=2 * ROWS), :],
                rows[pl.ds(ROWS + i, WAVES, stride=2 * ROWS), :],
            ],
            axis=0,
        )
        packed[i * 128 : (i + 1) * 128, :] = block.T

    for i in range(SLOTS // 2):
        lanes = slice(i * 128, (i + 1) * 128)
        m = m_ref[:, lanes]
        factor = jnp.where(m == 0, 1.0, 2.0).astype(f32)
        a, b, sign = rotation(m)
        parts = []
        for r in range(2):
            even = packed[(4 * i + r) * 72 : (4 * i + r + 1) * 72, :]
            odd = packed[(4 * i + 2 + r) * 72 : (4 * i + 3 + r) * 72, :]
            first = jnp.where(low, even, pltpu.roll(odd, 64, 1)) * factor
            second = jnp.where(low, pltpu.roll(even, 64, 1), odd) * factor
            parts.append((first, second))
        (re0, re1), (im0, im1) = parts
        for f in range(3):
            at = slice(f * 24, (f + 1) * 24)
            re = jnp.concatenate([re0[at], re1[at]], axis=0)
            im = jnp.concatenate([im0[at], im1[at]], axis=0)
            turned = [
                (re, im),
                (a * re - b * im, a * im + b * re),
                (sign * re, sign * im),
                (a * re + b * im, a * im - b * re),
            ]
            for r4 in range(4):
                out = slice(f * 192 + r4 * 48, f * 192 + (r4 + 1) * 48)
                coef[out, i * 128 : (i + 1) * 128] = turned[r4][0].astype(bf16)
                coef[out, MMAX + i * 128 : MMAX + (i + 1) * 128] = turned[r4][1].astype(bf16)


def inverse_kernel(points_ref, coef, flip, flux, keep_ref, send_ref, grid):
    lev = lax.axis_index("lev")
    points = points_ref[lev]
    quarter = points >> 2

    def transform(start, size):
        values = jnp.dot(
            coef[...], flip[:, pl.ds(start, size)], preferred_element_type=f32
        )
        index = start + lax.broadcasted_iota(jnp.int32, (192, size), 1)
        fields = [
            jnp.where(index < quarter, values[f * 192 : (f + 1) * 192], 0.0)
            .astype(bf16)
            .astype(f32)
            for f in range(3)
        ]
        products = [fields[0] * fields[2], fields[1] * fields[2], 0.5 * fields[2] * fields[2]]
        for f in range(3):
            flux[f * 192 : (f + 1) * 192, pl.ds(start, size)] = products[f].astype(bf16)
        for f in range(3):
            for r4 in range(4):
                grid[f, pl.ds(r4 * quarter + start, size), 0:48] = fields[f][
                    r4 * 48 : (r4 + 1) * 48
                ].T

    transform(QUARTER - 128, 128)

    def tile(step, carry):
        transform(pl.multiple_of((QUARTER // CHUNK - 1 - step) * CHUNK, CHUNK), CHUNK)
        return carry

    lax.fori_loop(0, QUARTER // CHUNK, tile, 0, unroll=5)

    chunk = 48
    for which, ref in ((0, keep_ref), (1, send_ref)):
        half = lev if which == 0 else 1 - lev

        def place(j, carry, half=half, ref=ref):
            lines = []
            for f in range(3):
                pieces = []
                for s in range(8):
                    first = half * HALF + j * (8 * chunk) + s
                    piece = grid[f, pl.ds(first, chunk, stride=8), :][:, 0:48]
                    place_of = first + 8 * lax.broadcasted_iota(jnp.int32, (chunk, 48), 0)
                    pieces.append(jnp.where(place_of < points, piece, 0.0))
                lines.append(jnp.concatenate(pieces, axis=1).astype(bf16))
            for f in range(3):
                ref[f, pl.ds(pl.multiple_of(j * chunk, 16), chunk), :] = lines[f]
            return carry

        lax.fori_loop(0, OUTR // chunk, place, 0, unroll=7)


def forward_kernel(weight_ref, m_ref, table, flux, ret_ref, rows, packed):
    low = lax.broadcasted_iota(jnp.int32, (72, 128), 1) < 64
    weight = weight_ref[lax.axis_index("lev")]

    for n in range(MMAX // CHUNK):
        at = n * CHUNK
        cos_sum = jnp.dot(flux[...], table[n, 0], preferred_element_type=f32)
        sin_sum = jnp.dot(flux[...], table[n, 1], preferred_element_type=f32)
        for i2 in range(2):
            lanes = slice(i2 * 128, (i2 + 1) * 128)
            a, b, sign = rotation(m_ref[:, pl.ds(at + i2 * 128, 128)])
            result = [[], []]
            for f in range(3):
                c = [cos_sum[f * 192 + r4 * 48 : f * 192 + (r4 + 1) * 48, lanes] for r4 in range(4)]
                s = [sin_sum[f * 192 + r4 * 48 : f * 192 + (r4 + 1) * 48, lanes] for r4 in range(4)]
                result[0].append(
                    (c[0] + sign * c[2] + a * (c[1] + c[3]) + b * (s[1] - s[3])) * weight
                )
                result[1].append(
                    (s[0] + sign * s[2] + a * (s[1] + s[3]) - b * (c[1] - c[3])) * weight
                )
            for r in range(2):
                first = jnp.concatenate([x[:24] for x in result[r]], axis=0)
                second = jnp.concatenate([x[24:] for x in result[r]], axis=0)
                row = (n * 8 + 4 * i2 + r) * 72
                packed[pl.ds(row, 72), :] = jnp.where(low, first, pltpu.roll(second, 64, 1))
                packed[pl.ds(row + 144, 72), :] = jnp.where(low, pltpu.roll(first, 64, 1), second)

    for i in range(ROWS):
        if i == ROWS - 1:
            block = jnp.zeros((128, 128), f32)
        else:
            block = packed[i * 128 : (i + 1) * 128, :].T
        rows[pl.ds(i, WAVES, stride=2 * ROWS), :] = block[:64]
        rows[pl.ds(ROWS + i, WAVES, stride=2 * ROWS), :] = block[64:]
    ret_ref[...] = rows[...].astype(bf16)


def unpack(payload, m_row):
    vmem = pl.BlockSpec(memory_space=pltpu.VMEM)
    return pl.pallas_call(
        unpack_kernel,
        in_specs=[vmem, vmem],
        out_specs=vmem,
        out_shape=jax.ShapeDtypeStruct((576, 2 * MMAX), bf16),
        scratch_shapes=[
            pltpu.VMEM((128 * ROWS, 128), f32),
            pltpu.VMEM((128 * ROWS, 128), f32),
        ],
        compiler_params=params(16),
        cost_estimate=pl.CostEstimate(flops=1 << 34, bytes_accessed=1 << 20, transcendentals=0),
        name="unpack",
    )(payload, m_row)


def inverse(points, coef, flip):
    vmem = pl.BlockSpec(memory_space=pltpu.VMEM)
    return pl.pallas_call(
        inverse_kernel,
        in_specs=[pl.BlockSpec(memory_space=pltpu.SMEM), vmem, vmem],
        out_specs=[vmem] * 3,
        out_shape=[
            jax.ShapeDtypeStruct((576, QUARTER), bf16),
            jax.ShapeDtypeStruct((3, OUTR, 384), bf16),
            jax.ShapeDtypeStruct((3, OUTR, 384), bf16),
        ],
        scratch_shapes=[pltpu.VMEM((3, 5264, 128), f32)],
        compiler_params=params(20),
        cost_estimate=pl.CostEstimate(
            flops=2 * QUARTER * 2 * MMAX * 576, bytes_accessed=12 << 20, transcendentals=0
        ),
        name="inverse",
    )(points, coef, flip)


def forward(weight, m_row, table, flux):
    vmem = pl.BlockSpec(memory_space=pltpu.VMEM)
    return pl.pallas_call(
        forward_kernel,
        in_specs=[
            pl.BlockSpec(memory_space=pltpu.SMEM), vmem, vmem, vmem
        ],
        out_specs=vmem,
        out_shape=jax.ShapeDtypeStruct((128 * ROWS, 128), bf16),
        scratch_shapes=[
            pltpu.VMEM((128 * ROWS, 128), f32),
            pltpu.VMEM((128 * ROWS, 128), f32),
        ],
        compiler_params=params(20),
        cost_estimate=pl.CostEstimate(
            flops=2 * QUARTER * 2 * MMAX * 576, bytes_accessed=12 << 20, transcendentals=0
        ),
        name="forward",
    )(weight, m_row, table, flux)


def local(spectra, legendre, block_slot, wavenumber, cycle_points, quad_weight):
    lev = lax.axis_index("lev")
    spec = jnp.transpose(spectra, (1, 0, 2))
    sent, order, counts = synthesis(block_slot, spec, legendre)
    sent = sent.reshape(128, ROWS, 128)
    received = lax.all_to_all(sent, ("wave", "lev"), split_axis=0, concat_axis=0, tiled=True)
    m_row = wavenumber.reshape(WAVES, SLOTS).T.reshape(1, MMAX)
    table, flip = tables(cycle_points, m_row)
    coef = unpack(received.reshape(128 * ROWS, 128), m_row)
    flux, keep, send = inverse(cycle_points, coef, flip)
    other = lax.ppermute(send, "lev", [(0, 1), (1, 0)])
    ret = forward(quad_weight, m_row, table, flux)
    returned = lax.all_to_all(
        ret.reshape(128, ROWS, 128), ("wave", "lev"), split_axis=0, concat_axis=0, tiled=True
    )
    arranged = arrange(order, counts, legendre)
    tendency = analysis(
        order, counts, returned.reshape(128 * ROWS, 128), arranged, legendre.shape[0]
    )
    own_first = lev == 0
    both = jnp.stack(
        [jnp.where(own_first, keep, other), jnp.where(own_first, other, keep)], axis=0
    )
    grid_fields = both[:, :, : HALF // 8, :].reshape(2, 3, HALF * 48)
    return (jnp.transpose(tendency, (1, 0, 2)), grid_fields)


def solution(mesh):
    placed = (P("wave", None, "lev"), P("wave", None, None), P("wave"), P(), P("wave"), P("wave"))
    return jax.shard_map(
        local,
        mesh=mesh,
        in_specs=placed,
        out_specs=(P("wave", None, "lev"), P("wave", None, "lev")),
        check_vma=False,
    )
```
